32 devices in a mesh: rows: 8 (over z, y), heads: 4 (over x, core).
Axes of the slice: x: 2, y: 2, z: 4, core: 2. Of those that a mesh axis runs over, the one named last changes fastest.
Arguments:
- tokens: bfloat16 [8, 2048, 768], P('rows', 'heads'), may hold values from -6 to 6
- lengths: int32 [8], P('rows'), may hold values from 8 to 2048, as said below
- w_qkv: bfloat16 [3, 768, 768], P(None, None, 'heads'), may hold values from -0.21875 to 0.21875
- w_out: bfloat16 [768, 768], P('heads'), may hold values from -1.25 to 1.25
- w_gate: bfloat16 [768, 3072], P(None, 'heads'), may hold values from -0.21875 to 0.21875
- w_up: bfloat16 [768, 3072], P(None, 'heads'), may hold values from -0.21875 to 0.21875
- w_down: bfloat16 [3072, 768], P('heads'), may hold values from -0.109375 to 0.109375
- gain_attn: float32 [768], replicated, may hold values from 0.25 to 1.75
- gain_mlp: float32 [768], replicated, may hold values from 0.25 to 1.75
- cotangent: bfloat16 [8, 2048, 768], P('rows', 'heads'), may hold values from -12 to 12
Outputs:
- layer_out: bfloat16 [8, 2048, 768], P('rows', 'heads')
- input_grad: bfloat16 [8, 2048, 768], P('rows', 'heads')
- grad_qkv: float32 [3, 768, 768], P(None, None, 'heads')
- grad_out: float32 [768, 768], P('heads')
- grad_gate: float32 [768, 3072], P(None, 'heads')
- grad_up: float32 [768, 3072], P(None, 'heads')
- grad_down: float32 [3072, 768], P('heads')
- grad_gain_attn: float32 [768], replicated
- grad_gain_mlp: float32 [768], replicated
The draws below stay inside these ranges and needn't reach their ends.
Inputs may be any that keep to these rules, and one draw needn't show every extreme that they name: `lengths`: in each aligned block of 1 row one row, chosen from the seed, has more than 1536 live tokens; at least one row has all 2048 positions live; the other rows are short ones of at most 64 tokens or longer ones of 64 or more.
All inputs are finite; a program needn't handle non-finite values.
Results may differ from the reference program's by a relative error of at most 0.02.
Values may be sent and summed in bfloat16 or wider, within the bound.
A program may use at most 128 MiB of HBM per device.

```python
import jax
import jax.numpy as jnp
from jax import lax

D = 768
HEADS = 12
HEAD = 64
FF = 3072
ROW_LEN = 2048
ROWS_GRP = 1
NSEQ = 8
N_HEADS = 4


def draw_lengths(key, part):
    groups = NSEQ // ROWS_GRP
    keys = jax.random.split(key, 6)
    kind = jax.random.randint(keys[0], (NSEQ,), 0, 2)
    short = jax.random.randint(keys[1], (NSEQ,), max(1, ROW_LEN // 256), ROW_LEN // 32 + 1)
    longer = jax.random.randint(keys[2], (NSEQ,), ROW_LEN // 32, ROW_LEN + 1)
    chosen = jnp.where(kind == 0, short, longer).reshape(groups, ROWS_GRP)
    pick = jax.random.randint(keys[3], (groups, 1), 0, ROWS_GRP)
    reaching = jax.random.randint(keys[4], (groups, 1), 3 * ROW_LEN // 4 + 1, ROW_LEN + 1)
    slot = jnp.arange(ROWS_GRP)[None, :]
    chosen = jnp.where(slot == pick, reaching, chosen).reshape(NSEQ)
    full_row = jax.random.randint(keys[5], (), 0, NSEQ)
    chosen = jnp.where(jnp.arange(NSEQ) == full_row, ROW_LEN, chosen)
    return chosen.astype(jnp.int32)


def draw_cotangent(key, part):
    first = jax.random.fold_in(key, 0)
    steps = jnp.arange(NSEQ).astype(jnp.float32) / max(NSEQ - 1, 1)
    rise = jnp.exp(jnp.log(3.0) * steps)[:, None, None]
    values = jnp.clip(jax.random.normal(first, (NSEQ, ROW_LEN, D), jnp.float32), -4.0, 4.0) * rise
    return values.astype(jnp.bfloat16)


def levels(rng, extent, pieces, smallest, top_value):
    def one(position, blocks):
        heights = jax.random.uniform(jax.random.fold_in(jax.random.fold_in(rng, 6), position), (blocks,), jnp.float32, smallest / len(pieces), top_value / len(pieces))
        return jnp.repeat(jnp.exp(heights), extent[position] // blocks).reshape((-1,) + (1,) * (len(extent) - position - 1))

    gain = one(*pieces[0])
    for cut in pieces[1:]:
        gain = gain * one(*cut)
    return gain


def centred(rng, dims, scale, reach, pieces=(), held_as=jnp.bfloat16):
    entries = scale * jax.random.normal(rng, dims, jnp.float32)
    if pieces:
        entries = entries * levels(rng, dims, pieces, -0.22, 0.18)
    return jnp.clip(entries, -reach, reach).astype(held_as)


def setup_inputs(seed: int = 0) -> dict:
    key_of = jax.random.split(jax.random.key(seed), 11)
    tokens = centred(key_of[0], (NSEQ, ROW_LEN, D), 1.0, 6.0, ((0, 8), (1, 4)))
    lengths = draw_lengths(jax.random.fold_in(key_of[10], 71), 0)
    w_qkv = centred(key_of[2], (3, D, D), D ** -0.5, 0.21875, ((2, 4),))
    w_out = centred(key_of[3], (D, D), (D // 32) ** -0.5, 1.25, ((0, 4),))
    w_gate = centred(key_of[4], (D, FF), D ** -0.5, 0.21875, ((1, 4),))
    w_up = centred(key_of[5], (D, FF), D ** -0.5, 0.21875, ((1, 4),))
    w_down = centred(key_of[6], (FF, D), FF ** -0.5, 0.109375, ((0, 4),))
    gain_attn = jnp.clip(1.0 + 0.15 * jax.random.normal(key_of[7], (D,), jnp.float32), 0.25, 1.75)
    gain_mlp = jnp.clip(1.0 + 0.15 * jax.random.normal(key_of[8], (D,), jnp.float32), 0.25, 1.75)
    cotangent = draw_cotangent(jax.random.fold_in(key_of[10], 71), 0)
    return dict(tokens=tokens, lengths=lengths, w_qkv=w_qkv, w_out=w_out, w_gate=w_gate, w_up=w_up, w_down=w_down, gain_attn=gain_attn, gain_mlp=gain_mlp, cotangent=cotangent)


eps = 1e-05
rope_base = 1000.0

@jax.custom_vjp
def low(v):
    return lax.optimization_barrier(v.astype(jnp.bfloat16)).astype(jnp.float32)

@jax.custom_vjp
def low_back(v):
    return v

def low_keep(v):
    return (low(v), None)

def low_pass(kept, grad):
    return (grad,)

def back_keep(v):
    return (v, None)

def back_low(kept, grad):
    return (low(grad),)
low.defvjp(low_keep, low_pass)
low_back.defvjp(back_keep, back_low)

def rotary_tables(length):
    half = HEAD // 2
    freqs = rope_base ** (-jnp.arange(half).astype(jnp.float32) / half)
    angles = jnp.arange(length).astype(jnp.float32)[:, None] * freqs[None, :]
    return (jnp.cos(angles), jnp.sin(angles))

def rotate(u, cosine, sine, sign):
    half = HEAD // 2
    first = u[..., :half]
    second = u[..., half:]
    cosine = cosine[None, :, None, :]
    sine = sine[None, :, None, :]
    return jnp.concatenate([first * cosine - sign * second * sine, second * cosine + sign * first * sine], axis=-1)

def layer_norm(resid):
    centre = resid - lax.optimization_barrier(jnp.mean(resid, axis=-1, keepdims=True))
    spread = lax.optimization_barrier(jnp.mean(centre * centre, axis=-1, keepdims=True))
    return centre * lax.rsqrt(spread + eps)

def forward(x, w_qkv, w_out, w_gate, w_up, w_down, gain_attn, gain_mlp, length):
    highest = lax.Precision.HIGHEST
    groups = N_HEADS
    per_group = HEADS // groups
    width = per_group * HEAD
    seq = x.shape[0]
    cosine, sine = rotary_tables(seq)
    x_groups = low_back(jnp.broadcast_to(x, (groups, seq, D)))
    weights = w_qkv.reshape(3, D, groups, width)
    proj = jnp.einsum('gld,cdge->cgle', x_groups, weights, precision=highest)
    proj = low_back(proj).reshape(3, groups, seq, per_group, HEAD)
    query = low(rotate(proj[0], cosine, sine, 1.0))
    key = low(rotate(proj[1], cosine, sine, 1.0))
    value = low(proj[2])
    scores = jnp.einsum('glhd,gkhd->ghlk', query, key, precision=highest) * 0.125
    scores = low_back(scores)
    valid = jnp.arange(seq).astype(jnp.int32) < length
    scores = jnp.where(valid[None, None, None, :], scores, -1e+30)
    top = lax.optimization_barrier(jnp.max(scores, axis=-1, keepdims=True))
    expo = jnp.exp(scores - top)
    probs = expo / lax.optimization_barrier(jnp.sum(expo, axis=-1, keepdims=True))
    attended = jnp.einsum('ghlk,gkhd->glhd', probs, value, precision=highest)
    attended = low(low_back(attended)).reshape(groups, seq, width)
    partial_attn = jnp.einsum('gle,ged->gld', attended, w_out.reshape(groups, width, D), precision=highest)
    attn = low_back(lax.optimization_barrier(jnp.sum(low(partial_attn), axis=0)))
    normed_one = layer_norm(x + attn) * gain_attn
    mlp_in = low_back(jnp.broadcast_to(low(normed_one), (groups, seq, D)))
    hidden_width = FF // groups
    gate = low_back(jnp.einsum('gld,dgf->glf', mlp_in, w_gate.reshape(D, groups, hidden_width), precision=highest))
    upper = low_back(jnp.einsum('gld,dgf->glf', mlp_in, w_up.reshape(D, groups, hidden_width), precision=highest))
    hidden = low(jax.nn.silu(gate) * upper)
    partial_mlp = jnp.einsum('glf,gfd->gld', hidden, w_down.reshape(groups, hidden_width, D), precision=highest)
    mlp = low_back(lax.optimization_barrier(jnp.sum(low(partial_mlp), axis=0)))
    return layer_norm(normed_one + mlp) * gain_mlp

def reference(tokens, lengths, w_qkv, w_out, w_gate, w_up, w_down, gain_attn, gain_mlp, cotangent):
    weights = (w_qkv.astype(jnp.float32), w_out.astype(jnp.float32), w_gate.astype(jnp.float32), w_up.astype(jnp.float32), w_down.astype(jnp.float32), gain_attn.astype(jnp.float32), gain_mlp.astype(jnp.float32))

    def per_row(carry, item):
        row_tokens, row_grad, length = item

        def apply_layer(xv, *params):
            return forward(xv, *params, length)
        result, pull = jax.vjp(apply_layer, row_tokens.astype(jnp.float32), *weights)
        grads = pull(row_grad.astype(jnp.float32))
        carry = tuple((total + grad for total, grad in zip(carry, grads[1:])))
        return (carry, (result.astype(jnp.bfloat16), grads[0].astype(jnp.bfloat16)))
    start = tuple((jnp.zeros(weight.shape, jnp.float32) for weight in weights))
    sums, (outputs, input_grads) = lax.scan(per_row, start, (tokens, cotangent, lengths))
    return (outputs, input_grads, sums[0], sums[1], sums[2], sums[3], sums[4], sums[5], sums[6])
```

```python
import functools

import jax
import jax.numpy as jnp
from jax import lax
from jax.experimental import pallas as pl
from jax.experimental.pallas import tpu as pltpu
from jax.sharding import PartitionSpec as P

HEAD = 64
eps = 1e-05
rope_base = 1000.0
MESH = pl.DeviceIdType.MESH
f32 = jnp.float32
bf16 = jnp.bfloat16
NCH = 4


def dot(a, b, ca=1, cb=0):
    return lax.dot_general(a, b, (((ca,), (cb,)), ((), ())), preferred_element_type=f32)


def mean(a):
    return jnp.mean(a, axis=-1, keepdims=True)


def layer_kernel(
    tok, cot, wqt_in, wo_in, wg_in, wu_in, wd_in, ga, gm, cos_t, sin_t, augk,
    out_y, out_dx, g_qkv, g_out, g_gate, g_up, g_down, g_ga, g_gm,
    xall, cotv, wqt, wo, wg, wu, wd, kt, vt, qn, qt, oall, x1b, rown, n1own, inv1own,
    act1, act2, hid, dmb, dab, mrecv, drecv, snd1, snd2, tmp, mtmp, dtmp, itmp,
    dkv, dkvr, dpt, ybuf,
    lsem, wss, wrs, xss, xrs, kss, krs, oss, ors, mss, mrs, bss, brs, dss, drs, ass_, ars,
    css, crs, fss, frs, gss, grs, gls, ysem, credit,
):
    length, width = tok.shape
    cl = length // NCH
    tq = 2 * cl
    ntok = 2 * length
    nkey = 2 * ntok
    qw = wo_in.shape[0]
    hc = qw // HEAD
    nh = 2 * hc
    npair = nh // 2
    fq = wg_in.shape[1]

    h = lax.axis_index("heads")
    x = h // 2
    c = h % 2
    oc = 1 - c
    ox = 1 - x
    core = {"heads": h + 1 - 2 * c}
    xp = {"heads": h + 2 - 4 * x}

    def remote(src, dst, ss, rs, dev):
        return pltpu.make_async_remote_copy(
            src_ref=src, dst_ref=dst, send_sem=ss, recv_sem=rs, device_id=dev, device_id_type=MESH
        )

    barrier = pltpu.get_barrier_semaphore()
    for dev in (core, xp):
        pl.semaphore_signal(barrier, inc=1, device_id=dev, device_id_type=MESH)

    def local_copies():
        cps = []
        for i in range(NCH):
            cps.append(pltpu.make_async_copy(tok.at[pl.ds(i * cl, cl)], xall.at[i, x], lsem.at[i]))
        n = NCH
        for src, dst in (
            (wqt_in, wqt.at[c]), (wo_in, wo.at[x, pl.ds(c * qw, qw)]), (wg_in, wg.at[c]),
            (wu_in, wu.at[c]), (wd_in, wd.at[c]), (cot, cotv),
        ):
            cps.append(pltpu.make_async_copy(src, dst, lsem.at[n]))
            n += 1
        return cps

    locals_ = local_copies()
    for cp in locals_:
        cp.start()

    pl.semaphore_wait(barrier, 2)

    def xcopy(i):
        return remote(tok.at[pl.ds(i * cl, cl)], xall.at[i, x], xss.at[i], xrs.at[i], xp)

    w_q = remote(wqt_in, wqt.at[c], wss.at[0], wrs.at[0], core)
    w_o = remote(wo_in, wo.at[x, pl.ds(c * qw, qw)], wss.at[1], wrs.at[1], core)
    w_ox = remote(wo_in, wo.at[x, pl.ds(c * qw, qw)], wss.at[2], wrs.at[2], xp)
    w_oxc = remote(
        wo.at[ox, pl.ds(c * qw, qw)], wo.at[ox, pl.ds(c * qw, qw)], wss.at[3], wrs.at[3], core
    )
    w_g = remote(wg_in, wg.at[c], wss.at[4], wrs.at[4], core)
    w_u = remote(wu_in, wu.at[c], wss.at[5], wrs.at[5], core)
    w_d = remote(wd_in, wd.at[c], wss.at[6], wrs.at[6], core)
    w_q.start()
    for i in range(NCH):
        xcopy(i).start()
    w_o.start()
    w_g.start()
    w_u.start()
    w_d.start()
    w_ox.start()

    nrow = lax.broadcasted_iota(jnp.int32, (HEAD, nkey), 0)
    vrows = jnp.where(nrow < 2, 1.0, 0.0).astype(bf16)
    for pr in range(npair):
        kt[pr, 0, HEAD:, :] = augk[...]
        kt[pr, 1, :HEAD, :] = augk[...]
        vt[pr, 0, HEAD:, :] = vrows
        vt[pr, 1, :HEAD, :] = vrows
    dkv[...] = jnp.zeros_like(dkv)
    g_ga[...] = jnp.zeros_like(g_ga)
    g_gm[...] = jnp.zeros_like(g_gm)

    lane = lax.broadcasted_iota(jnp.int32, (tq, 2 * HEAD), 1)
    low_half = lane < HEAD

    def rotate(u, cs, sn, sign):
        half = HEAD // 2
        a, b = u[:half], u[half:]
        return jnp.concatenate([a * cs - sign * (b * sn), b * cs + sign * (a * sn)], axis=0)

    def kvcopies(i):
        cps = []
        cols = pl.ds(pl.multiple_of(c * ntok + i * tq, tq), tq)
        n = 0
        for ref in (kt, vt):
            for par in range(2):
                part = ref.at[:, par, pl.ds(par * HEAD, HEAD), cols]
                cps.append(remote(part, part, kss.at[i, n], krs.at[i, n], core))
                n += 1
        return cps

    locals_[NCH].wait()
    w_q.wait_recv()

    def qkv(i, carry):
        pltpu.make_async_copy(tok.at[pl.ds(i * cl, cl)], xall.at[i, x], lsem.at[i]).wait()
        xcopy(i).wait_recv()
        xb = xall[i].reshape(tq, width)
        here = pl.ds(pl.multiple_of(i * tq, tq), tq)
        cols = pl.ds(pl.multiple_of(c * ntok + i * tq, tq), tq)
        cs = cos_t[:, here]
        sn = sin_t[:, here]
        for cc in range(2):
            pt = dot(wqt[cc], xb, 1, 1)
            for j in range(hc):
                hh = cc * hc + j
                pr, par = hh // 2, hh % 2
                at = slice(par * HEAD, par * HEAD + HEAD)
                q = rotate(pt[j * HEAD : (j + 1) * HEAD], cs, sn, 1.0).astype(bf16)
                qt[hh, :, here] = (q.astype(f32) * 0.125).astype(bf16)
                k = rotate(pt[qw + j * HEAD : qw + (j + 1) * HEAD], cs, sn, 1.0)
                kt[pr, par, at, cols] = k.astype(bf16)
                vt[pr, par, at, cols] = pt[2 * qw + j * HEAD : 2 * qw + (j + 1) * HEAD].astype(bf16)
        for cp in kvcopies(i):
            cp.start()
        for pr in range(npair):
            both = jnp.concatenate([qt[2 * pr, :, here], qt[2 * pr + 1, :, here]], axis=0)
            nat = both.astype(f32).T
            qn[2 * pr, here, :] = jnp.where(
                low_half, nat, jnp.where(lane == HEAD, 1.0, 0.0)
            ).astype(bf16)
            qn[2 * pr + 1, here, :] = jnp.where(
                low_half, jnp.where(lane == 0, 1.0, 0.0), nat
            ).astype(bf16)
        return carry

    lax.fori_loop(0, NCH, qkv, 0)

    def kvwait(i, carry):
        for cp in kvcopies(i):
            cp.wait_recv()
        return carry

    lax.fori_loop(0, NCH, kvwait, 0)
    w_ox.wait_recv()
    w_oxc.start()
    for cp in locals_[NCH + 1 :]:
        cp.wait()
    for w in (w_o, w_oxc, w_g, w_u, w_d):
        w.wait_recv()

    def rows_of(i):
        return pl.ds(pl.multiple_of(i * tq, tq), tq)

    def own_of(i):
        return pl.ds(pl.multiple_of(i * cl, cl), cl)

    def ocopy(i):
        part = oall.at[x, rows_of(i)]
        return remote(part, part, oss.at[i], ors.at[i], xp)

    def mcopy(i):
        return remote(snd1.at[i], mrecv.at[i], mss.at[i], mrs.at[i], xp)

    def bcopy(i):
        return remote(dmb.at[i, x], dmb.at[i, x], bss.at[i], brs.at[i], xp)

    def dcopy(i):
        return remote(snd2.at[i], drecv.at[i], dss.at[i], drs.at[i], xp)

    def acopy(i):
        return remote(dab.at[i, x], dab.at[i, x], ass_.at[i], ars.at[i], xp)

    def ycopy(i):
        return pltpu.make_async_copy(ybuf.at[i], out_y.at[pl.ds(i * cl, cl)], ysem.at[i])

    def attend(i):
        rows = rows_of(i)
        for pr in range(npair):
            outs = []
            for par in range(2):
                hh = 2 * pr + par
                base = HEAD * (1 - par)
                qq = qn[hh, rows, :]
                s = dot(qq, kt[pr, par])
                top = jnp.max(s, axis=1, keepdims=True)
                p = jnp.exp(s - top).astype(bf16)
                oo = dot(p, vt[pr, par], 1, 1)
                total = oo[:, base : base + 1]
                outs.append(oo * (1.0 / total))
                neg = -(top + jnp.log(total))
                hi = neg.astype(bf16).astype(f32)
                mid = (neg - hi).astype(bf16).astype(f32)
                lo = neg - hi - mid
                qf = qq.astype(f32)
                qf = jnp.where(lane == base + 1, hi, qf)
                qf = jnp.where(lane == base + 2, mid, qf)
                qf = jnp.where(lane == base + 3, lo, qf)
                qn[hh, rows, :] = qf.astype(bf16)
            oall[x, rows, pr * 2 * HEAD : (pr + 1) * 2 * HEAD] = jnp.where(
                low_half, outs[0], outs[1]
            ).astype(bf16)
        ocopy(i).start()

    def mlp_fwd(i):
        rows, own = rows_of(i), own_of(i)
        ocopy(i).wait_recv()
        a = dot(oall[0, rows, :], wo[0]) + dot(oall[1, rows, :], wo[1])
        r = xall[i].reshape(tq, width).astype(f32) + a
        centre = r - mean(r)
        inv = lax.rsqrt(mean(centre * centre) + eps)
        n1 = centre * inv
        tmp[...] = n1.reshape(2, cl, width)
        n1own[own, :] = tmp[x]
        itmp[...] = jnp.broadcast_to(inv, (tq, 128)).reshape(2, cl, 128)
        inv1own[own, :] = itmp[x]
        x1 = n1 * ga[...]
        tmp[...] = x1.reshape(2, cl, width)
        rown[own, :] = tmp[x]
        xb = x1.astype(bf16)
        x1b[rows, :] = xb
        m = None
        for cc in range(2):
            g = dot(xb, wg[cc])
            u = dot(xb, wu[cc])
            sg = 0.5 * jnp.tanh(0.5 * g) + 0.5
            si = g * sg
            hv = (si * u).astype(bf16)
            act2[cc, rows, :] = si.astype(bf16)
            act1[cc, rows, :] = (u * (sg + si * (1.0 - sg))).astype(bf16)
            hid[cc, rows, :] = hv
            part = dot(hv, wd[cc])
            m = part if m is None else m + part
        mtmp[...] = m.reshape(2, cl, width)
        snd1[i] = mtmp[ox].astype(bf16)
        mcopy(i).start()

    def norm_two(i):
        own = own_of(i)
        mcopy(i).wait_recv()
        r = rown[own, :] + (mtmp[x] + mrecv[i].astype(f32))
        centre = r - mean(r)
        inv = lax.rsqrt(mean(centre * centre) + eps)
        n2 = centre * inv
        ybuf[i] = (n2 * gm[...]).astype(bf16)
        ycopy(i).start()
        dy = cotv[own, :].astype(f32)
        g_gm[...] += jnp.sum(dy * n2, axis=0, keepdims=True)
        e = dy * gm[...]
        dr = inv * (e - mean(e) - n2 * mean(e * n2))
        rown[own, :] = dr
        dmb[i, x] = dr.astype(bf16)
        bcopy(i).start()

    def mlp_bwd(i):
        rows = rows_of(i)
        bcopy(i).wait_recv()
        db = dmb[i].reshape(tq, width)
        d = None
        for cc in range(2):
            dh = dot(db, wd[cc], 1, 1)
            dg = (dh * act1[cc, rows, :].astype(f32)).astype(bf16)
            du = (dh * act2[cc, rows, :].astype(f32)).astype(bf16)
            act1[cc, rows, :] = dg
            act2[cc, rows, :] = du
            part = dot(dg, wg[cc], 1, 1) + dot(du, wu[cc], 1, 1)
            d = part if d is None else d + part
        dtmp[...] = d.reshape(2, cl, width)
        snd2[i] = dtmp[ox].astype(bf16)
        dcopy(i).start()

    def norm_one(i):
        own = own_of(i)
        dcopy(i).wait_recv()
        dx = rown[own, :] + (dtmp[x] + drecv[i].astype(f32))
        n1 = n1own[own, :]
        g_ga[...] += jnp.sum(dx * n1, axis=0, keepdims=True)
        e = dx * ga[...]
        dr = inv1own[own, 0:1] * (e - mean(e) - n1 * mean(e * n1))
        rown[own, :] = dr
        dab[i, x] = dr.astype(bf16)
        acopy(i).start()

    kb = min(1024, nkey)

    def attend_back(i):
        rows = rows_of(i)
        acopy(i).wait_recv()
        da = dab[i].reshape(tq, width)
        cs = cos_t[:, rows]
        sn = sin_t[:, rows]
        wox = wo[x]
        for pr in range(npair):
            pair = slice(pr * 2 * HEAD, (pr + 1) * 2 * HEAD)
            dop = dot(da, wox[pair], 1, 1).astype(bf16)
            dof = dop.astype(f32)
            prod = dof * oall[x, rows, pair].astype(f32)
            dot_t = dof.T.astype(bf16)
            dqs = []
            for par in range(2):
                hh = 2 * pr + par
                base = HEAD * (1 - par)
                mine = low_half if par == 0 else jnp.logical_not(low_half)
                neg = -jnp.sum(jnp.where(mine, prod, 0.0), axis=1, keepdims=True)
                hi = neg.astype(bf16).astype(f32)
                lo = neg - hi
                aug = jnp.where(lane == base, hi, jnp.where(lane == base + 1, lo, 0.0))
                doa = jnp.where(mine, dof, aug).astype(bf16)
                qq = qn[hh, rows, :]
                dq = None
                for b in range(nkey // kb):
                    kk = slice(b * kb, (b + 1) * kb)
                    p = jnp.exp(dot(qq, kt[pr, par, :, kk]))
                    d = dot(doa, vt[pr, par, :, kk])
                    ds = (p * d).astype(bf16)
                    pb = p.astype(bf16)
                    dkv[1, hh, :, kk] += dot(dot_t[par * HEAD : (par + 1) * HEAD], pb)
                    dkv[0, hh, :, kk] += dot(qt[hh, :, rows], ds)
                    part = dot(ds, kt[pr, par, :, kk], 1, 1)
                    dq = part if dq is None else dq + part
                dqs.append(dq)
            dqt = jnp.where(low_half, dqs[0], dqs[1]).T * 0.125
            for par in range(2):
                hh = 2 * pr + par
                cc, j = hh // hc, hh % hc
                u = rotate(dqt[par * HEAD : (par + 1) * HEAD], cs, sn, -1.0)
                dpt[cc, j * HEAD : (j + 1) * HEAD, rows] = u.astype(bf16)

    stages = (attend, mlp_fwd, norm_two, mlp_bwd, norm_one, attend_back)

    def step(t, carry):
        for lag in reversed(range(len(stages))):
            stage = stages[lag]

            @pl.when(jnp.logical_and(t >= lag, t < NCH + lag))
            def _():
                stage(t - lag)

        return carry

    lax.fori_loop(0, NCH + len(stages) - 1, step, 0)

    def give_credit(n):
        pl.semaphore_signal(credit.at[n], inc=1, device_id=core, device_id_type=MESH)

    blk = pl.ds(0, fq)
    out_rows = pl.ds(0, qw)
    qkv_rows = pl.ds(qw, 3 * qw)
    g_plan = (
        (wg.at[0], wg.at[1], wd.at[1], g_gate),
        (wu.at[0], wu.at[1], act1.at[0, blk], g_up),
        (wd.at[0], act1.at[1, blk], act2.at[0, blk], g_down),
        (act2.at[1, out_rows], hid.at[1, out_rows], hid.at[0, out_rows], g_out),
        (act2.at[1, qkv_rows], hid.at[1, qkv_rows], hid.at[0, qkv_rows], g_qkv),
    )

    def gcopy(n):
        return remote(g_plan[n][2], g_plan[n][1], gss.at[n], grs.at[n], core)

    def gstore(n):
        return pltpu.make_async_copy(g_plan[n][0], g_plan[n][3], gls.at[n])

    def gsum(n):
        gcopy(n).wait()
        mine, got = g_plan[n][:2]
        mine[...] = (mine[...].astype(f32) + got[...].astype(f32)).astype(bf16)
        gstore(n).start()

    dmball = dmb[...].reshape(ntok, width)
    g_plan[0][2][...] = dot(x1b[...], act1[oc], 0, 0).astype(bf16)
    g_plan[0][0][...] = dot(x1b[...], act1[c], 0, 0).astype(bf16)
    give_credit(0)
    pl.semaphore_wait(credit.at[0], 1)
    gcopy(0).start()
    g_plan[1][2][...] = dot(x1b[...], act2[oc], 0, 0).astype(bf16)
    gcopy(1).start()
    g_plan[1][0][...] = dot(x1b[...], act2[c], 0, 0).astype(bf16)
    g_plan[2][2][...] = dot(hid[oc], dmball, 0, 0).astype(bf16)
    gcopy(2).start()
    g_plan[2][0][...] = dot(hid[c], dmball, 0, 0).astype(bf16)
    give_credit(1)
    pl.semaphore_wait(credit.at[1], 1)
    for n in range(3):
        gsum(n)

    theirs = pl.ds(pl.multiple_of(oc * ntok, ntok), ntok)
    mine_cols = pl.ds(pl.multiple_of(c * ntok, ntok), ntok)
    for hh in range(nh):
        cc, j = hh // hc, hh % hc
        for n in range(2):
            at = slice((n + 1) * qw + j * HEAD, (n + 1) * qw + (j + 1) * HEAD)
            dpt[cc, at, :] = dkv[n, hh, :, theirs].astype(bf16)
    kvback = remote(dpt.at[:, pl.ds(qw, 2 * qw)], dkvr, css.at[0], crs.at[0], core)
    kvback.start()

    daball = dab[...].reshape(ntok, width)
    o = oall[x]
    part_a = dot(o[:, :qw], daball, 0, 0)
    part_b = dot(o[:, qw:], daball, 0, 0)
    g_plan[3][2][...] = jnp.where(oc == 0, part_a, part_b).astype(bf16)
    gcopy(3).start()
    g_plan[3][0][...] = jnp.where(c == 0, part_a, part_b).astype(bf16)

    kvback.wait()
    for hh in range(nh):
        cc, j = hh // hc, hh % hc
        for n in range(2):
            at = slice((n + 1) * qw + j * HEAD, (n + 1) * qw + (j + 1) * HEAD)
            got = slice(n * qw + j * HEAD, n * qw + (j + 1) * HEAD)
            u = dkv[n, hh, :, mine_cols] + dkvr[cc, got].astype(f32)
            if n == 0:
                u = rotate(u, cos_t[...], sin_t[...], -1.0)
            dpt[cc, at, :] = u.astype(bf16)

    def fcopy(i):
        return remote(snd1.at[i], mrecv.at[i], fss.at[i], frs.at[i], xp)

    def input_terms(i, who):
        cols = pl.ds(pl.multiple_of(i * tq + who * cl, cl), cl)
        d = None
        for cc in range(2):
            part = dot(dpt[cc, :, cols], wqt[cc], 0, 0)
            d = part if d is None else d + part
        return d

    for i in range(NCH):
        mcopy(i).wait_send()
        snd1[i] = input_terms(i, ox).astype(bf16)
        fcopy(i).start()

    xr = xall[...].reshape(ntok, width)
    g_plan[4][2][...] = dot(dpt[oc], xr).astype(bf16)
    gcopy(4).start()
    g_plan[4][0][...] = dot(dpt[c], xr).astype(bf16)
    gsum(3)
    gsum(4)

    for i in range(NCH):
        d = input_terms(i, x)
        fcopy(i).wait_recv()
        own = pl.ds(i * cl, cl)
        d = rown[own, :] + (d + mrecv[i].astype(f32))
        ycopy(i).wait()
        ybuf[i] = d.astype(bf16)
        pltpu.make_async_copy(ybuf.at[i], out_dx.at[own], lsem.at[i]).start()

    for i in range(NCH):
        own = pl.ds(i * cl, cl)
        pltpu.make_async_copy(ybuf.at[i], out_dx.at[own], lsem.at[i]).wait()
        xcopy(i).wait_send()
        for cp in kvcopies(i):
            cp.wait_send()
        ocopy(i).wait_send()
        bcopy(i).wait_send()
        dcopy(i).wait_send()
        acopy(i).wait_send()
        fcopy(i).wait_send()
    for w in (w_q, w_o, w_ox, w_oxc, w_g, w_u, w_d):
        w.wait_send()
    for n in range(len(g_plan)):
        gstore(n).wait()


def on_device(tokens, lengths, w_qkv, w_out, w_gate, w_up, w_down, gain_attn, gain_mlp, cotangent):
    _, length, width = tokens.shape
    qw = w_qkv.shape[2]
    fq = w_gate.shape[1]
    nh = 2 * qw // HEAD
    cl = length // NCH
    tq = 2 * cl
    ntok = 2 * length
    nkey = 2 * ntok
    h = lax.axis_index("heads")
    c = h % 2

    order = jnp.arange(nkey, dtype=jnp.int32).reshape(2, NCH, 2, cl)
    cores = lax.broadcasted_iota(jnp.int32, order.shape, 0)
    chunk = lax.broadcasted_iota(jnp.int32, order.shape, 1)
    xs = lax.broadcasted_iota(jnp.int32, order.shape, 2)
    place = lax.broadcasted_iota(jnp.int32, order.shape, 3)
    position = (2 * xs + cores) * length + chunk * cl + place
    valid = position.reshape(1, nkey) < lengths[0]
    row = lax.broadcasted_iota(jnp.int32, (HEAD, nkey), 0)
    augk = jnp.where(
        row == 0, jnp.where(valid, 0.0, -1e30), jnp.where(row < 4, 1.0, 0.0)
    ).astype(bf16)
    here = ((2 * xs[0] + c) * length + chunk[0] * cl + place[0]).reshape(1, ntok).astype(f32)
    half = HEAD // 2
    freqs = rope_base ** (-jnp.arange(half).astype(f32) / half)
    angles = freqs[:, None] * here
    cos_t, sin_t = jnp.cos(angles), jnp.sin(angles)

    wqt = w_qkv.transpose(0, 2, 1).reshape(3 * qw, width)

    hbm = pl.BlockSpec(memory_space=pl.ANY)
    vmem = pl.BlockSpec(memory_space=pltpu.VMEM)
    S = jax.ShapeDtypeStruct
    V = pltpu.VMEM
    dma = pltpu.SemaphoreType.DMA
    fc = 2 * fq
    scratch = [
        V((NCH, 2, cl, width), bf16),
        V((length, width), bf16),
        V((2, 3 * qw, width), bf16),
        V((2, 2 * qw, width), bf16),
        V((2, width, fq), bf16),
        V((2, width, fq), bf16),
        V((2, fq, width), bf16),
        V((nh // 2, 2, 2 * HEAD, nkey), bf16),
        V((nh // 2, 2, 2 * HEAD, nkey), bf16),
        V((nh, ntok, 2 * HEAD), bf16),
        V((nh, HEAD, ntok), bf16),
        V((2, ntok, 2 * qw), bf16),
        V((ntok, width), bf16),
        V((length, width), f32),
        V((length, width), f32),
        V((length, 128), f32),
        V((2, ntok, fq), bf16),
        V((2, ntok, fq), bf16),
        V((2, ntok, fq), bf16),
        V((NCH, 2, cl, width), bf16),
        V((NCH, 2, cl, width), bf16),
        V((NCH, cl, width), bf16),
        V((NCH, cl, width), bf16),
        V((NCH, cl, width), bf16),
        V((NCH, cl, width), bf16),
        V((2, cl, width), f32),
        V((2, cl, width), f32),
        V((2, cl, width), f32),
        V((2, cl, 128), f32),
        V((2, nh, HEAD, nkey), f32),
        V((2, 2 * qw, ntok), bf16),
        V((2, 3 * qw, ntok), bf16),
        V((NCH, cl, width), bf16),
        dma((NCH + 6,)),
        dma((7,)), dma((7,)),
        dma((NCH,)), dma((NCH,)),
        dma((NCH, 4)), dma((NCH, 4)),
        dma((NCH,)), dma((NCH,)),
        dma((NCH,)), dma((NCH,)),
        dma((NCH,)), dma((NCH,)),
        dma((NCH,)), dma((NCH,)),
        dma((NCH,)), dma((NCH,)),
        dma((1,)), dma((1,)),
        dma((NCH,)), dma((NCH,)),
        dma((5,)), dma((5,)), dma((5,)),
        dma((NCH,)),
        pltpu.SemaphoreType.REGULAR((2,)),
    ]
    outs = pl.pallas_call(
        layer_kernel,
        out_shape=[
            S((length, width), bf16), S((length, width), bf16),
            S((3 * qw, width), bf16), S((qw, width), bf16),
            S((width, fq), bf16), S((width, fq), bf16), S((fq, width), bf16),
            S((1, width), f32), S((1, width), f32),
        ],
        in_specs=[hbm] * 7 + [vmem] * 5,
        out_specs=[hbm] * 7 + [vmem] * 2,
        scratch_shapes=scratch,
        compiler_params=pltpu.CompilerParams(
            collective_id=0, has_side_effects=True, vmem_limit_bytes=VLIM
        ),
    )(
        tokens[0], cotangent[0], wqt, w_out, w_gate, w_up, w_down,
        gain_attn[None], gain_mlp[None], cos_t, sin_t, augk,
    )
    y, dx, gqt, go, gg, gu, gd, gga, ggm = outs
    gqt, go, gg, gu, gd = lax.psum((gqt, go, gg, gu, gd), "rows")
    gga, ggm = lax.psum((gga, ggm), ("rows", "heads"))
    grad_qkv = gqt.astype(f32).reshape(3, qw, width).transpose(0, 2, 1)
    return (
        y[None], dx[None], grad_qkv, go.astype(f32), gg.astype(f32), gu.astype(f32),
        gd.astype(f32), gga[0], ggm[0],
    )


VLIM = 64 * 2**20


def solution(mesh):
    in_specs = (
        P("rows", "heads", None),
        P("rows"),
        P(None, None, "heads"),
        P("heads", None),
        P(None, "heads"),
        P(None, "heads"),
        P("heads", None),
        P(),
        P(),
        P("rows", "heads", None),
    )
    out_specs = (
        P("rows", "heads", None),
        P("rows", "heads", None),
        P(None, None, "heads"),
        P("heads", None),
        P(None, "heads"),
        P(None, "heads"),
        P("heads", None),
        P(),
        P(),
    )
    return jax.shard_map(
        on_device, mesh=mesh, in_specs=in_specs, out_specs=out_specs, check_vma=False
    )
```

```python
import functools

import jax
import jax.numpy as jnp
from jax import lax
from jax.experimental import pallas as pl
from jax.experimental.pallas import tpu as pltpu
from jax.sharding import PartitionSpec as P

HEAD = 64
eps = 1e-05
rope_base = 1000.0
MESH = pl.DeviceIdType.MESH
f32 = jnp.float32
bf16 = jnp.bfloat16
NCH = 4


def dot(a, b, ca=1, cb=0):
    return lax.dot_general(a, b, (((ca,), (cb,)), ((), ())), preferred_element_type=f32)


def mean(a):
    return jnp.mean(a, axis=-1, keepdims=True)


def layer_kernel(
    nrows, tok, cot, wqt_in, wo_in, wg_in, wu_in, wd_in, ga, gm, cos_t, sin_t, augk,
    out_y, out_dx, g_mlp, g_att, g_gain,
    xall, cotv, wqt, wo, wm, kt, vt, qn, qt, oall, x1b, rown, n1own, inv1own,
    act1, act2, hid, dmb, dab, mrecv, drecv, snd1, snd2, tmp, mtmp, dtmp, itmp,
    dkv, dkvr, dpt, ybuf, gsent, agrad, gbuf, grecv,
    lsem, wss, wrs, xss, xrs, kss, krs, oss, ors, mss, mrs, bss, brs, dss, drs, ass_, ars,
    css, crs, fss, frs, gss, grs, gls, rss, rrs, fas, far, ns, nr, ysem, credit,
):
    ring = nrows == 8
    length, width = tok.shape
    cl = length // NCH
    tq = 2 * cl
    ntok = 2 * length
    nkey = 2 * ntok
    hc = wo_in.shape[0]
    qw = hc * HEAD
    fq = wg_in.shape[1]

    h = lax.axis_index("heads")
    r = lax.axis_index("rows")
    x = h // 2
    c = h % 2
    oc = 1 - c
    ox = 1 - x
    core = {"heads": h + 1 - 2 * c}
    xp = {"heads": h + 2 - 4 * x}
    y = r % 2
    z = r // 2
    outer = jnp.logical_or(z == 0, z == 3)
    inner = jnp.logical_not(outer)
    ydev = {"rows": r + 1 - 2 * y}
    zdev = {"rows": r + 2 - 4 * (z % 2)}
    mid = {"rows": (3 - z) * 2 + y}
    doubling = [core, xp]
    span = 1
    while span < nrows:
        doubling.append({"rows": r + span - 2 * span * ((r // span) % 2)})
        span *= 2

    def when(cond):
        return pl.when(cond)

    def remote(src, dst, ss, rs, dev):
        return pltpu.make_async_remote_copy(
            src_ref=src, dst_ref=dst, send_sem=ss, recv_sem=rs, device_id=dev, device_id_type=MESH
        )

    barrier = pltpu.get_barrier_semaphore()
    for dev in doubling:
        pl.semaphore_signal(barrier, inc=1, device_id=dev, device_id_type=MESH)
    greeted = len(doubling)
    if ring:

        @when(inner)
        def _():
            pl.semaphore_signal(barrier, inc=1, device_id=mid, device_id_type=MESH)

        greeted = greeted + jnp.where(inner, 1, 0)

    def local_copies():
        cps = []
        for i in range(NCH):
            cps.append(pltpu.make_async_copy(tok.at[pl.ds(i * cl, cl)], xall.at[i, x], lsem.at[i]))
        n = NCH
        for src, dst in (
            (wqt_in, wqt.at[c]), (wo_in, wo.at[x, :, c]), (wg_in, wm.at[3 * c]),
            (wu_in, wm.at[3 * c + 1]), (wd_in, wm.at[3 * c + 2]), (cot, cotv),
        ):
            cps.append(pltpu.make_async_copy(src, dst, lsem.at[n]))
            n += 1
        return cps

    locals_ = local_copies()
    for cp in locals_:
        cp.start()

    pl.semaphore_wait(barrier, greeted)

    def xcopy(i):
        return remote(tok.at[pl.ds(i * cl, cl)], xall.at[i, x], xss.at[i], xrs.at[i], xp)

    w_q = remote(wqt_in, wqt.at[c], wss.at[0], wrs.at[0], core)
    w_o = remote(wo_in, wo.at[x, :, c], wss.at[1], wrs.at[1], core)
    w_ox = remote(wo_in, wo.at[x, :, c], wss.at[2], wrs.at[2], xp)
    w_oxc = remote(wo.at[ox, :, c], wo.at[ox, :, c], wss.at[3], wrs.at[3], core)
    w_g = remote(wg_in, wm.at[3 * c], wss.at[4], wrs.at[4], core)
    w_u = remote(wu_in, wm.at[3 * c + 1], wss.at[5], wrs.at[5], core)
    w_d = remote(wd_in, wm.at[3 * c + 2], wss.at[6], wrs.at[6], core)
    w_q.start()
    for i in range(NCH):
        xcopy(i).start()
    w_o.start()
    w_g.start()
    w_u.start()
    w_d.start()
    w_ox.start()

    nrow = lax.broadcasted_iota(jnp.int32, (HEAD, nkey), 0)
    vrows = jnp.where(nrow < 2, 1.0, 0.0).astype(bf16)
    for pr in range(hc):
        kt[pr, 0, HEAD:, :] = augk[...]
        kt[pr, 1, :HEAD, :] = augk[...]
        vt[pr, 0, HEAD:, :] = vrows
        vt[pr, 1, :HEAD, :] = vrows
    gbuf[...] = jnp.zeros_like(gbuf)

    lane = lax.broadcasted_iota(jnp.int32, (tq, 2 * HEAD), 1)
    low_half = lane < HEAD

    def rotate(u, cs, sn, sign):
        half = HEAD // 2
        a, b = u[:half], u[half:]
        return jnp.concatenate([a * cs - sign * (b * sn), b * cs + sign * (a * sn)], axis=0)

    def kvcopies(i):
        cps = []
        cols = pl.ds(pl.multiple_of(c * ntok + i * tq, tq), tq)
        n = 0
        for ref in (kt, vt):
            for par in range(2):
                part = ref.at[:, par, pl.ds(par * HEAD, HEAD), cols]
                cps.append(remote(part, part, kss.at[i, n], krs.at[i, n], core))
                n += 1
        return cps

    locals_[NCH].wait()
    w_q.wait_recv()

    def qkv(i, carry):
        pltpu.make_async_copy(tok.at[pl.ds(i * cl, cl)], xall.at[i, x], lsem.at[i]).wait()
        xcopy(i).wait_recv()
        xb = xall[i].reshape(tq, width)
        here = pl.ds(pl.multiple_of(i * tq, tq), tq)
        cols = pl.ds(pl.multiple_of(c * ntok + i * tq, tq), tq)
        cs = cos_t[:, here]
        sn = sin_t[:, here]
        for cc in range(2):
            pt = dot(wqt[cc], xb, 1, 1)
            at = slice(cc * HEAD, cc * HEAD + HEAD)
            for j in range(hc):
                u = pt[j * 3 * HEAD : (j + 1) * 3 * HEAD]
                q = rotate(u[:HEAD], cs, sn, 1.0).astype(bf16)
                qt[cc, j, :, here] = (q.astype(f32) * 0.125).astype(bf16)
                kt[j, cc, at, cols] = rotate(u[HEAD : 2 * HEAD], cs, sn, 1.0).astype(bf16)
                vt[j, cc, at, cols] = u[2 * HEAD :].astype(bf16)
        for cp in kvcopies(i):
            cp.start()
        for j in range(hc):
            both = jnp.concatenate([qt[0, j, :, here], qt[1, j, :, here]], axis=0)
            nat = both.astype(f32).T
            qn[0, j, here, :] = jnp.where(
                low_half, nat, jnp.where(lane == HEAD, 1.0, 0.0)
            ).astype(bf16)
            qn[1, j, here, :] = jnp.where(
                low_half, jnp.where(lane == 0, 1.0, 0.0), nat
            ).astype(bf16)
        return carry

    lax.fori_loop(0, NCH, qkv, 0)

    def kvwait(i, carry):
        for cp in kvcopies(i):
            cp.wait_recv()
        return carry

    lax.fori_loop(0, NCH, kvwait, 0)
    w_ox.wait_recv()
    w_oxc.start()
    for cp in locals_[NCH + 1 :]:
        cp.wait()
    for w in (w_o, w_oxc, w_g, w_u, w_d):
        w.wait_recv()

    def rows_of(i):
        return pl.ds(pl.multiple_of(i * tq, tq), tq)

    def hid_rows(cc, i):
        return pl.ds(pl.multiple_of(cc * ntok + i * tq, tq), tq)

    def own_of(i):
        return pl.ds(pl.multiple_of(i * cl, cl), cl)

    def ocopy(i):
        part = oall.at[x, rows_of(i)]
        return remote(part, part, oss.at[i], ors.at[i], xp)

    def mcopy(i):
        return remote(snd1.at[i], mrecv.at[i], mss.at[i], mrs.at[i], xp)

    def bcopy(i):
        return remote(dmb.at[i, x], dmb.at[i, x], bss.at[i], brs.at[i], xp)

    def dcopy(i):
        return remote(snd2.at[i], drecv.at[i], dss.at[i], drs.at[i], xp)

    def acopy(i):
        return remote(dab.at[i, x], dab.at[i, x], ass_.at[i], ars.at[i], xp)

    def ycopy(i):
        return pltpu.make_async_copy(ybuf.at[i], out_y.at[pl.ds(i * cl, cl)], ysem.at[i])

    def attend(i):
        rows = rows_of(i)
        for j in range(hc):
            outs = []
            for par in range(2):
                base = HEAD * (1 - par)
                qq = qn[par, j, rows, :]
                s = dot(qq, kt[j, par])
                top = jnp.max(s, axis=1, keepdims=True)
                p = jnp.exp(s - top).astype(bf16)
                oo = dot(p, vt[j, par], 1, 1)
                total = oo[:, base : base + 1]
                outs.append(oo * (1.0 / total))
                neg = -(top + jnp.log(total))
                hi = neg.astype(bf16).astype(f32)
                mid = (neg - hi).astype(bf16).astype(f32)
                lo = neg - hi - mid
                qf = qq.astype(f32)
                qf = jnp.where(lane == base + 1, hi, qf)
                qf = jnp.where(lane == base + 2, mid, qf)
                qf = jnp.where(lane == base + 3, lo, qf)
                qn[par, j, rows, :] = qf.astype(bf16)
            oall[x, rows, j * 2 * HEAD : (j + 1) * 2 * HEAD] = jnp.where(
                low_half, outs[0], outs[1]
            ).astype(bf16)
        ocopy(i).start()

    def mlp_fwd(i):
        rows, own = rows_of(i), own_of(i)
        ocopy(i).wait_recv()
        a = dot(oall[0, rows, :], wo[0].reshape(2 * qw, width))
        a += dot(oall[1, rows, :], wo[1].reshape(2 * qw, width))
        r = xall[i].reshape(tq, width).astype(f32) + a
        centre = r - mean(r)
        inv = lax.rsqrt(mean(centre * centre) + eps)
        n1 = centre * inv
        tmp[...] = n1.reshape(2, cl, width)
        n1own[own, :] = tmp[x]
        itmp[...] = jnp.broadcast_to(inv, (tq, 128)).reshape(2, cl, 128)
        inv1own[own, :] = itmp[x]
        x1 = n1 * ga[...]
        tmp[...] = x1.reshape(2, cl, width)
        rown[own, :] = tmp[x]
        xb = x1.astype(bf16)
        x1b[rows, :] = xb
        m = None
        for cc in range(2):
            g = dot(xb, wm[3 * cc])
            u = dot(xb, wm[3 * cc + 1])
            sg = 0.5 * jnp.tanh(0.5 * g) + 0.5
            si = g * sg
            hv = (si * u).astype(bf16)
            at = hid_rows(cc, i)
            act2[at, :] = si.astype(bf16)
            act1[at, :] = (u * (sg + si * (1.0 - sg))).astype(bf16)
            hid[at, :] = hv
            part = dot(hv, wm[3 * cc + 2])
            m = part if m is None else m + part
        mtmp[...] = m.reshape(2, cl, width)
        snd1[i] = mtmp[ox].astype(bf16)
        mcopy(i).start()

    def norm_two(i):
        own = own_of(i)
        mcopy(i).wait_recv()
        r = rown[own, :] + (mtmp[x] + mrecv[i].astype(f32))
        centre = r - mean(r)
        inv = lax.rsqrt(mean(centre * centre) + eps)
        n2 = centre * inv
        ybuf[i] = (n2 * gm[...]).astype(bf16)
        ycopy(i).start()
        dy = cotv[own, :].astype(f32)
        gbuf[1:2, :] += jnp.sum(dy * n2, axis=0, keepdims=True)
        e = dy * gm[...]
        dr = inv * (e - mean(e) - n2 * mean(e * n2))
        rown[own, :] = dr
        dmb[i, x] = dr.astype(bf16)
        bcopy(i).start()

    def mlp_bwd(i):
        bcopy(i).wait_recv()
        db = dmb[i].reshape(tq, width)
        d = None
        for cc in range(2):
            at = hid_rows(cc, i)
            dh = dot(db, wm[3 * cc + 2], 1, 1)
            dg = (dh * act1[at, :].astype(f32)).astype(bf16)
            du = (dh * act2[at, :].astype(f32)).astype(bf16)
            act1[at, :] = dg
            act2[at, :] = du
            part = dot(dg, wm[3 * cc], 1, 1) + dot(du, wm[3 * cc + 1], 1, 1)
            d = part if d is None else d + part
        dtmp[...] = d.reshape(2, cl, width)
        snd2[i] = dtmp[ox].astype(bf16)
        dcopy(i).start()

    def norm_one(i):
        own = own_of(i)
        dcopy(i).wait_recv()
        dx = rown[own, :] + (dtmp[x] + drecv[i].astype(f32))
        n1 = n1own[own, :]
        gbuf[0:1, :] += jnp.sum(dx * n1, axis=0, keepdims=True)
        e = dx * ga[...]
        dr = inv1own[own, 0:1] * (e - mean(e) - n1 * mean(e * n1))
        rown[own, :] = dr
        dab[i, x] = dr.astype(bf16)
        acopy(i).start()

    kb = min(1024, nkey)

    def attend_back(j, i):
        rows = rows_of(i)

        @when(j == 0)
        def _():
            acopy(i).wait_recv()

        @when(i == 0)
        def _():
            dkv[j % 2] = jnp.zeros(dkv.shape[1:], f32)

        da = dab[i].reshape(tq, width)
        cs = cos_t[:, rows]
        sn = sin_t[:, rows]
        lanes = pl.ds(pl.multiple_of(j * 2 * HEAD, 2 * HEAD), 2 * HEAD)
        dop = dot(da, wo[x, j].reshape(2 * HEAD, width), 1, 1).astype(bf16)
        dof = dop.astype(f32)
        prod = dof * oall[x, rows, lanes].astype(f32)
        dot_t = dof.T.astype(bf16)
        dqs = []
        for par in range(2):
            base = HEAD * (1 - par)
            mine = low_half if par == 0 else jnp.logical_not(low_half)
            neg = -jnp.sum(jnp.where(mine, prod, 0.0), axis=1, keepdims=True)
            hi = neg.astype(bf16).astype(f32)
            lo = neg - hi
            aug = jnp.where(lane == base, hi, jnp.where(lane == base + 1, lo, 0.0))
            doa = jnp.where(mine, dof, aug).astype(bf16)
            qq = qn[par, j, rows, :]
            dq = None
            for b in range(nkey // kb):
                kk = slice(b * kb, (b + 1) * kb)
                p = jnp.exp(dot(qq, kt[j, par, :, kk]))
                d = dot(doa, vt[j, par, :, kk])
                ds = (p * d).astype(bf16)
                pb = p.astype(bf16)
                dkv[j % 2, par, HEAD:, kk] += dot(dot_t[par * HEAD : (par + 1) * HEAD], pb)
                dkv[j % 2, par, :HEAD, kk] += dot(qt[par, j, :, rows], ds)
                part = dot(ds, kt[j, par, :, kk], 1, 1)
                dq = part if dq is None else dq + part
            dqs.append(dq)
        dqt = jnp.where(low_half, dqs[0], dqs[1]).T * 0.125
        at = pl.ds(pl.multiple_of(j * 3 * HEAD, HEAD), HEAD)
        for par in range(2):
            u = rotate(dqt[par * HEAD : (par + 1) * HEAD], cs, sn, -1.0)
            dpt[par, at, rows] = u.astype(bf16)

    stages = (attend, mlp_fwd, norm_two, mlp_bwd, norm_one)

    def step(t, carry):
        for lag in reversed(range(len(stages))):
            stage = stages[lag]

            @when(jnp.logical_and(t >= lag, t < NCH + lag))
            def _():
                stage(t - lag)

        return carry

    lax.fori_loop(0, NCH + 2, step, 0)

    blk = pl.ds(0, fq)
    blk2 = pl.ds(fq, fq)
    g_sent = (gsent, act1.at[blk], act1.at[blk2])

    def gcopy(n):
        return remote(g_sent[n], wm.at[3 + n], gss.at[n], grs.at[n], core)

    def gsum(n):
        gcopy(n).wait()
        wm[n] = (wm[n].astype(f32) + wm[3 + n].astype(f32)).astype(bf16)

    def give(n, dev):
        pl.semaphore_signal(credit.at[n], inc=1, device_id=dev, device_id_type=MESH)

    def half_of(ref, cc):
        return ref[pl.ds(pl.multiple_of(cc * ntok, ntok), ntok), :]

    def mlp_grads():
        norm_one(NCH - 2)
        mlp_bwd(NCH - 1)
        give(0, core)
        gsent[...] = dot(x1b[...], half_of(act1, oc), 0, 0).astype(bf16)
        wm[0] = dot(x1b[...], half_of(act1, c), 0, 0).astype(bf16)
        act1[blk, :] = dot(x1b[...], half_of(act2, oc), 0, 0).astype(bf16)
        pl.semaphore_wait(credit.at[0], 1)
        gcopy(0).start()
        gcopy(1).start()
        wm[1] = dot(x1b[...], half_of(act2, c), 0, 0).astype(bf16)
        dmball = dmb[...].reshape(ntok, width)
        act1[blk2, :] = dot(half_of(hid, oc), dmball, 0, 0).astype(bf16)
        gcopy(2).start()
        wm[2] = dot(half_of(hid, c), dmball, 0, 0).astype(bf16)
        give(1, core)
        for i in range(NCH):
            bcopy(i).wait_send()
        if ring:
            give(2, ydev)
            give(2, zdev)

            @when(inner)
            def _():
                give(2, mid)

        norm_one(NCH - 1)
        for n in range(3):
            gsum(n)
        pl.semaphore_wait(credit.at[1], 1)
        if ring:
            pl.semaphore_wait(credit.at[2], 2 + jnp.where(inner, 1, 0))

    place = jnp.where(y == 0, z, 7 - z)
    seg = fq // 16
    hops = 14

    def ring_row(p):
        p = (p + 8) % 8
        return {"rows": jnp.where(p < 4, 2 * p, 15 - 2 * p)}

    def ring_copies(u, k, to_slot):
        cps = []
        for d in range(2):
            sign = 1 - 2 * d
            at = d * 8 * seg + ((place - sign * k + 16) % 8) * seg
            rows = pl.ds(pl.multiple_of(at, 16), seg)
            if to_slot:
                slot = ((u * 2 + d) * 7 + k) * seg
                part = wm.at[u, rows]
                dst = act2.at[pl.ds(pl.multiple_of(slot, 16), seg)]
            else:
                part = dst = wm.at[3 + u, rows]
            cps.append(
                remote(part, dst, rss.at[u, d, k], rrs.at[u, d, k], ring_row(place + sign))
            )
        return cps

    def ring_step(m):
        u, k = m % 3, m // 3

        @when(k >= 1)
        def _():
            for cp in ring_copies(u, k - 1, False):
                cp.wait_recv()

        @when(jnp.logical_and(k >= 1, k <= 7))
        def _():
            for d in range(2):
                sign = 1 - 2 * d
                at = d * 8 * seg + ((place - sign * k + 16) % 8) * seg
                rows = pl.ds(pl.multiple_of(at, 16), seg)
                slot = pl.ds(pl.multiple_of(((u * 2 + d) * 7 + k - 1) * seg, 16), seg)
                wm[jnp.where(k == 7, 3 + u, u), rows, :] = (
                    wm[u, rows, :].astype(f32) + act2[slot, :].astype(f32)
                ).astype(bf16)

        @when(k <= 6)
        def _():
            for cp in ring_copies(u, k, True):
                cp.start()

        @when(jnp.logical_and(k >= 7, k < hops))
        def _():
            for cp in ring_copies(u, k, False):
                cp.start()

        @when(k >= 2)
        def _():
            for cp in ring_copies(u, k - 2, False):
                cp.wait_send()

    sub = 3 * HEAD

    def acore(b):
        src = hid.at[pl.ds(pl.multiple_of((4 + b) * sub, sub), sub)]
        dst = hid.at[pl.ds(pl.multiple_of(b * sub, sub), sub)]
        return remote(src, dst, gss.at[3 + b], grs.at[3 + b], core)

    def asum(b):
        acore(b).wait()
        got = hid[pl.ds(pl.multiple_of(b * sub, sub), sub), :]
        rows = pl.ds(pl.multiple_of(b * sub, sub), sub)
        agrad[rows, :] = (agrad[rows, :].astype(f32) + got.astype(f32)).astype(bf16)

    def astart(b, theirs, ours):
        hid[pl.ds(pl.multiple_of((4 + b) * sub, sub), sub), :] = theirs.astype(bf16)
        acore(b).start()
        agrad[pl.ds(pl.multiple_of(b * sub, sub), sub), :] = ours.astype(bf16)

    hs = sub // 2

    def tree(b, phase):
        mine = agrad.at[pl.ds(pl.multiple_of(b * sub + y * hs, hs), hs)]
        final = hid.at[pl.ds(pl.multiple_of(b * sub + y * hs, hs), hs)]
        buf_a = x1b.at[pl.ds(b * sub, hs)]
        buf_b = x1b.at[pl.ds(b * sub + hs, hs)]
        buf_c = dmb.at[b, 0, pl.ds(0, hs)]
        c0 = lambda: remote(agrad.at[pl.ds(pl.multiple_of(b * sub + (1 - y) * hs, hs), hs)], buf_a, fas.at[b, 0], far.at[b, 0], ydev)
        c1 = lambda: remote(mine, buf_b, fas.at[b, 1], far.at[b, 1], zdev)
        c2 = lambda: remote(mine, buf_c, fas.at[b, 2], far.at[b, 2], mid)
        c3 = lambda: remote(final, final, fas.at[b, 3], far.at[b, 3], zdev)
        c4 = lambda: remote(final, final, fas.at[b, 4], far.at[b, 4], ydev)

        def add(buf, dst):
            dst[...] = (mine[...].astype(f32) + buf[...].astype(f32)).astype(bf16)

        if phase == 0:
            c0().start()
        elif phase == 1:
            c0().wait_recv()
            add(buf_a, mine)

            @when(outer)
            def _():
                c1().start()
        elif phase == 2:

            @when(inner)
            def _():
                c1().wait_recv()
                add(buf_b, mine)
                c2().start()
        elif phase == 3:

            @when(inner)
            def _():
                c2().wait()
                add(buf_c, final)
                c3().start()
                c4().start()
        elif phase == 4:

            @when(outer)
            def _():
                c3().wait_recv()
                c4().start()
        else:
            c4().wait_recv()
            c0().wait_send()
            c4().wait_send()

            @when(outer)
            def _():
                c1().wait_send()

            @when(inner)
            def _():
                c3().wait_send()

    def gain_copy(n):
        return remote(gbuf, grecv.at[n], ns.at[n], nr.at[n], doubling[n])

    def gain_step(n):
        if n > 0:
            gain_copy(n - 1).wait()
            gbuf[...] += grecv[n - 1]
        if n < len(doubling):
            gain_copy(n).start()

    theirs_cols = pl.ds(pl.multiple_of(oc * ntok, ntok), ntok)
    mine_cols = pl.ds(pl.multiple_of(c * ntok, ntok), ntok)

    def kv_rows(j):
        return pl.ds(pl.multiple_of(j * 3 * HEAD + HEAD, HEAD), 2 * HEAD)

    def kvback(j):
        return remote(dpt.at[:, kv_rows(j)], dkvr.at[j], css.at[j], crs.at[j], core)

    def kv_send(j):
        dpt[:, kv_rows(j), :] = dkv[j % 2, :, :, theirs_cols].astype(bf16)
        kvback(j).start()

    def kv_finish(j):
        kvback(j).wait()
        base = j * 3 * HEAD
        for par in range(2):
            u = dkv[j % 2, par, :, mine_cols] + dkvr[j, par].astype(f32)
            dk = rotate(u[:HEAD], cos_t[...], sin_t[...], -1.0)
            dpt[par, pl.ds(pl.multiple_of(base + HEAD, HEAD), HEAD), :] = dk.astype(bf16)
            dpt[par, pl.ds(pl.multiple_of(base + 2 * HEAD, HEAD), HEAD), :] = u[HEAD:].astype(bf16)

    def qkv_grads(j):
        rows = pl.ds(pl.multiple_of(j * sub, HEAD), sub)
        xr = xall[...].reshape(ntok, width)
        astart(1 + j, dot(dpt[oc, rows, :], xr), dot(dpt[c, rows, :], xr))

    def out_grads():
        both = dot(oall[x], dab[...].reshape(ntok, width), 0, 0).reshape(hc, 2, HEAD, width)
        first = both[:, 0].reshape(sub, width)
        second = both[:, 1].reshape(sub, width)
        astart(0, jnp.where(c == 0, second, first), jnp.where(c == 0, first, second))

    def at_step(q, n):
        return when(q == n)

    def back(q, carry):
        j, i = q // NCH, q % NCH
        attend_back(j, i)

        @at_step(q, 0)
        def _():
            mlp_grads()

        @when(i == NCH - 1)
        def _():
            @when(j < hc - 1)
            def _():
                kv_send(j)

        @when(jnp.logical_and(i == 0, j > 0))
        def _():
            kv_finish(j - 1)
            qkv_grads(j - 1)

        @at_step(q, 3)
        def _():
            out_grads()

        @at_step(q, 4)
        def _():
            asum(0)

        @when(jnp.logical_and(i == 1, j > 0))
        def _():
            asum(j)

        for n in range(len(doubling) + 1):

            @at_step(q, min(2 + n, NCH * hc - 1))
            def _():
                gain_step(n)

        if ring:
            for b, ph, n in TREE_PLAN:

                @at_step(q, n)
                def _():
                    tree(b, ph)

            for extra in range(2):
                ring_step(2 * q + extra)
        return carry

    lax.fori_loop(0, NCH * hc, back, 0)

    def fcopy(i):
        return remote(snd1.at[i], mrecv.at[i], fss.at[i], frs.at[i], xp)

    def input_terms(i, who):
        cols = pl.ds(pl.multiple_of(i * tq + who * cl, cl), cl)
        d = None
        for cc in range(2):
            part = dot(dpt[cc, :, cols], wqt[cc], 0, 0)
            d = part if d is None else d + part
        return d

    def rings(first, last):
        if ring:

            def one(m, carry):
                ring_step(m)
                return carry

            lax.fori_loop(first, last, one, 0)

    def trees(*steps):
        if ring:
            for b, ph in steps:
                tree(b, ph)

    last = hc - 1
    done = 2 * NCH * hc
    kv_send(last)
    trees((2, 2), (0, 5), (1, 4))
    rings(done, done + 2)
    kv_finish(last)
    for i in range(NCH):
        mcopy(i).wait_send()
        snd1[i] = input_terms(i, ox).astype(bf16)
        fcopy(i).start()
    qkv_grads(last)
    rings(done + 2, done + 4)
    asum(1 + last)
    trees((3, 0), (2, 3), (1, 5))
    rings(done + 4, done + 7)
    trees((3, 1), (2, 4))
    rings(done + 7, done + 10)
    trees((3, 2), (2, 5))
    rings(done + 10, done + 13)
    trees((3, 3))
    rings(done + 13, done + 16)
    trees((3, 4))

    for i in range(NCH):
        d = input_terms(i, x)
        fcopy(i).wait_recv()
        own = pl.ds(i * cl, cl)
        d = rown[own, :] + (d + mrecv[i].astype(f32))
        ycopy(i).wait()
        ybuf[i] = d.astype(bf16)
        pltpu.make_async_copy(ybuf.at[i], out_dx.at[own], lsem.at[i]).start()
    rings(done + 16, 3 * (hops + 1))
    trees((3, 5))

    def result_copies():
        return [
            pltpu.make_async_copy(wm.at[pl.ds(3 if ring else 0, 3)], g_mlp, gls.at[0]),
            pltpu.make_async_copy(
                hid.at[pl.ds(0, (1 + hc) * sub)] if ring else agrad, g_att, gls.at[1]
            ),
        ]

    for cp in result_copies():
        cp.start()
    g_gain[...] = gbuf[...]

    for i in range(NCH):
        own = pl.ds(i * cl, cl)
        pltpu.make_async_copy(ybuf.at[i], out_dx.at[own], lsem.at[i]).wait()
        xcopy(i).wait_send()
        for cp in kvcopies(i):
            cp.wait_send()
        ocopy(i).wait_send()
        dcopy(i).wait_send()
        acopy(i).wait_send()
        fcopy(i).wait_send()
    for w in (w_q, w_o, w_ox, w_oxc, w_g, w_u, w_d):
        w.wait_send()
    if ring:
        for u in range(3):
            for cp in ring_copies(u, hops - 1, False):
                cp.wait_send()
    for cp in result_copies():
        cp.wait()


TREE_PLAN = (
    (0, 0, 4), (0, 1, 6), (0, 2, 8), (0, 3, 10), (0, 4, 11),
    (1, 0, 5), (1, 1, 7), (1, 2, 9), (1, 3, 11),
    (2, 0, 9), (2, 1, 11),
)


def on_device(
    nrows, tokens, lengths, w_qkv, w_out, w_gate, w_up, w_down, gain_attn, gain_mlp, cotangent
):
    _, length, width = tokens.shape
    qw = w_qkv.shape[2]
    fq = w_gate.shape[1]
    hc = qw // HEAD
    nh = 2 * hc
    cl = length // NCH
    tq = 2 * cl
    ntok = 2 * length
    nkey = 2 * ntok
    h = lax.axis_index("heads")
    c = h % 2

    order = jnp.arange(nkey, dtype=jnp.int32).reshape(2, NCH, 2, cl)
    cores = lax.broadcasted_iota(jnp.int32, order.shape, 0)
    chunk = lax.broadcasted_iota(jnp.int32, order.shape, 1)
    xs = lax.broadcasted_iota(jnp.int32, order.shape, 2)
    place = lax.broadcasted_iota(jnp.int32, order.shape, 3)
    position = (2 * xs + cores) * length + chunk * cl + place
    valid = position.reshape(1, nkey) < lengths[0]
    row = lax.broadcasted_iota(jnp.int32, (HEAD, nkey), 0)
    augk = jnp.where(
        row == 0, jnp.where(valid, 0.0, -1e30), jnp.where(row < 4, 1.0, 0.0)
    ).astype(bf16)
    here = ((2 * xs[0] + c) * length + chunk[0] * cl + place[0]).reshape(1, ntok).astype(f32)
    half = HEAD // 2
    freqs = rope_base ** (-jnp.arange(half).astype(f32) / half)
    angles = freqs[:, None] * here
    cos_t, sin_t = jnp.cos(angles), jnp.sin(angles)

    wqt = w_qkv.reshape(3, width, hc, HEAD).transpose(2, 0, 3, 1).reshape(3 * qw, width)

    hbm = pl.BlockSpec(memory_space=pl.ANY)
    vmem = pl.BlockSpec(memory_space=pltpu.VMEM)
    S = jax.ShapeDtypeStruct
    V = pltpu.VMEM
    dma = pltpu.SemaphoreType.DMA
    doublings = 2 + (nrows - 1).bit_length()
    scratch = [
        V((NCH, 2, cl, width), bf16),
        V((length, width), bf16),
        V((2, 3 * qw, width), bf16),
        V((2, hc, 2, HEAD, width), bf16),
        V((6, width, fq), bf16),
        V((hc, 2, 2 * HEAD, nkey), bf16),
        V((hc, 2, 2 * HEAD, nkey), bf16),
        V((2, hc, ntok, 2 * HEAD), bf16),
        V((2, hc, HEAD, ntok), bf16),
        V((2, ntok, 2 * qw), bf16),
        V((ntok, width), bf16),
        V((length, width), f32),
        V((length, width), f32),
        V((length, 128), f32),
        V((2 * ntok, fq), bf16),
        V((2 * ntok, fq), bf16),
        V((2 * ntok, fq), bf16),
        V((NCH, 2, cl, width), bf16),
        V((NCH, 2, cl, width), bf16),
        V((NCH, cl, width), bf16),
        V((NCH, cl, width), bf16),
        V((NCH, cl, width), bf16),
        V((NCH, cl, width), bf16),
        V((2, cl, width), f32),
        V((2, cl, width), f32),
        V((2, cl, width), f32),
        V((2, cl, 128), f32),
        V((2, 2, 2 * HEAD, nkey), f32),
        V((hc, 2, 2 * HEAD, ntok), bf16),
        V((2, 3 * qw, ntok), bf16),
        V((NCH, cl, width), bf16),
        V((width, fq), bf16),
        V(((1 + hc) * 3 * HEAD, width), bf16),
        V((8, width), f32),
        V((doublings, 8, width), f32),
        dma((NCH + 6,)),
        dma((7,)), dma((7,)),
        dma((NCH,)), dma((NCH,)),
        dma((NCH, 4)), dma((NCH, 4)),
        dma((NCH,)), dma((NCH,)),
        dma((NCH,)), dma((NCH,)),
        dma((NCH,)), dma((NCH,)),
        dma((NCH,)), dma((NCH,)),
        dma((NCH,)), dma((NCH,)),
        dma((hc,)), dma((hc,)),
        dma((NCH,)), dma((NCH,)),
        dma((4 + hc,)), dma((4 + hc,)), dma((2,)),
        dma((3, 2, 14)), dma((3, 2, 14)),
        dma((1 + hc, 5)), dma((1 + hc, 5)),
        dma((doublings,)), dma((doublings,)),
        dma((NCH,)),
        pltpu.SemaphoreType.REGULAR((3,)),
    ]
    outs = pl.pallas_call(
        functools.partial(layer_kernel, nrows),
        out_shape=[
            S((length, width), bf16), S((length, width), bf16),
            S((3, width, fq), bf16), S(((1 + hc) * 3 * HEAD, width), bf16), S((8, width), f32),
        ],
        in_specs=[hbm] * 7 + [vmem] * 5,
        out_specs=[hbm] * 4 + [vmem],
        scratch_shapes=scratch,
        compiler_params=pltpu.CompilerParams(
            collective_id=0, has_side_effects=True, vmem_limit_bytes=VLIM
        ),
    )(
        tokens[0], cotangent[0], wqt, w_out.reshape(hc, HEAD, width), w_gate, w_up, w_down,
        gain_attn[None], gain_mlp[None], cos_t, sin_t, augk,
    )
    y, dx, g_mlp, g_att, g_gain = outs
    if nrows != 8:
        g_mlp, g_att = lax.psum((g_mlp, g_att), "rows")
    g_att = g_att.reshape(1 + hc, 3 * HEAD, width)
    grad_qkv = g_att[1:].reshape(hc, 3, HEAD, width).transpose(1, 3, 0, 2)
    return (
        y[None], dx[None], grad_qkv.astype(f32).reshape(3, width, qw), g_att[0].astype(f32),
        g_mlp[0].astype(f32), g_mlp[1].astype(f32), g_mlp[2].astype(f32), g_gain[0], g_gain[1],
    )


VLIM = 64 * 2**20


def solution(mesh):
    in_specs = (
        P("rows", "heads", None),
        P("rows"),
        P(None, None, "heads"),
        P("heads", None),
        P(None, "heads"),
        P(None, "heads"),
        P("heads", None),
        P(),
        P(),
        P("rows", "heads", None),
    )
    out_specs = (
        P("rows", "heads", None),
        P("rows", "heads", None),
        P(None, None, "heads"),
        P("heads", None),
        P(None, "heads"),
        P(None, "heads"),
        P("heads", None),
        P(),
        P(),
    )
    return jax.shard_map(
        functools.partial(on_device, mesh.shape["rows"]), mesh=mesh, in_specs=in_specs, out_specs=out_specs, check_vma=False
    )
```

```python
import functools

import jax
import jax.numpy as jnp
import numpy as np
from jax import lax
from jax.experimental import pallas as pl
from jax.experimental.pallas import tpu as pltpu
from jax.sharding import PartitionSpec as P

HEAD = 64
eps = 1e-05
rope_base = 1000.0
MESH = pl.DeviceIdType.MESH
f32 = jnp.float32
bf16 = jnp.bfloat16
NCH = 4


def dot(a, b, ca=1, cb=0):
    return lax.dot_general(a, b, (((ca,), (cb,)), ((), ())), preferred_element_type=f32)


def mean(a):
    return jnp.mean(a, axis=-1, keepdims=True)


def layer_kernel(
    nrows, tok, cot, wq_in, wo_in, wg_in, wu_in, wd_in, turns, lengths, ga_in, gm_in, place_in,
    out_y, out_dx, g_mlp, g_out, g_qkv, g_ga, g_gm,
    xall, cotv, wqt, wo, wm, kt, vt, qn, qt, oall, x1b, rown, n1own, inv1own,
    act1, act2, hid, dmb, dab, mrecv, drecv, snd1, snd2, tmp, itmp,
    dkv, dkvr, dpt, ybuf, agrad, gbuf, grecv, turn,
    lsem, wqs, wqr, wss, wrs, xss, xrs, kss, krs, oss, ors, mss, mrs, bss, brs, dss, drs, ass_, ars,
    css, crs, fss, frs, gss, grs, gls, rss, rrs, fas, far, ns, nr, ysem, credit,
):
    ring = nrows == 8
    length, width = tok.shape
    cl = length // NCH
    tq = 2 * cl
    ntok = 2 * length
    nkey = 2 * ntok
    hc = wo_in.shape[0]
    qw = hc * HEAD
    fq = wg_in.shape[1]

    h = lax.axis_index("heads")
    r = lax.axis_index("rows")
    x = h // 2
    c = h % 2
    oc = 1 - c
    ox = 1 - x
    core = {"heads": h + 1 - 2 * c}
    xp = {"heads": h + 2 - 4 * x}
    y = r % 2
    z = r // 2
    outer = jnp.logical_or(z == 0, z == 3)
    inner = jnp.logical_not(outer)
    ydev = {"rows": r + 1 - 2 * y}
    zdev = {"rows": r + 2 - 4 * (z % 2)}
    mid = {"rows": (3 - z) * 2 + y}
    doubling = [core, xp]
    span = 1
    while span < nrows:
        doubling.append({"rows": r + span - 2 * span * ((r // span) % 2)})
        span *= 2

    def when(cond):
        return pl.when(cond)

    def remote(src, dst, ss, rs, dev):
        return pltpu.make_async_remote_copy(
            src_ref=src, dst_ref=dst, send_sem=ss, recv_sem=rs, device_id=dev, device_id_type=MESH
        )

    barrier = pltpu.get_barrier_semaphore()
    for dev in doubling:
        pl.semaphore_signal(barrier, inc=1, device_id=dev, device_id_type=MESH)
    greeted = len(doubling)
    if ring:

        @when(inner)
        def _():
            pl.semaphore_signal(barrier, inc=1, device_id=mid, device_id_type=MESH)

        greeted = greeted + jnp.where(inner, 1, 0)

    def local_copies():
        cps = []
        for i in range(NCH):
            cps.append(pltpu.make_async_copy(tok.at[pl.ds(i * cl, cl)], xall.at[i, x], lsem.at[i]))
        n = NCH
        for src, dst in (
            (wq_in.at[0], wqt.at[c, :, 0]), (wq_in.at[1], wqt.at[c, :, 1]),
            (wq_in.at[2], wqt.at[c, :, 2]), (turns.at[c], turn), (wo_in, wo.at[x, :, c]), (wg_in, wm.at[3 * c]),
            (wu_in, wm.at[3 * c + 1]), (wd_in, wm.at[3 * c + 2]), (cot, cotv),
        ):
            cps.append(pltpu.make_async_copy(src, dst, lsem.at[n]))
            n += 1
        return cps

    locals_ = local_copies()
    for cp in locals_:
        cp.start()

    pl.semaphore_wait(barrier, greeted)

    def xcopy(i):
        return remote(tok.at[pl.ds(i * cl, cl)], xall.at[i, x], xss.at[i], xrs.at[i], xp)

    w_q = [
        remote(wq_in.at[n], wqt.at[c, :, n], wqs.at[n], wqr.at[n], core) for n in range(3)
    ]
    w_o = remote(wo_in, wo.at[x, :, c], wss.at[1], wrs.at[1], core)
    w_ox = remote(wo_in, wo.at[x, :, c], wss.at[2], wrs.at[2], xp)
    w_oxc = remote(wo.at[ox, :, c], wo.at[ox, :, c], wss.at[3], wrs.at[3], core)
    w_g = remote(wg_in, wm.at[3 * c], wss.at[4], wrs.at[4], core)
    w_u = remote(wu_in, wm.at[3 * c + 1], wss.at[5], wrs.at[5], core)
    w_d = remote(wd_in, wm.at[3 * c + 2], wss.at[6], wrs.at[6], core)
    for w in w_q:
        w.start()
    for i in range(NCH):
        xcopy(i).start()
    w_o.start()
    w_g.start()
    w_u.start()
    w_d.start()
    w_ox.start()

    nrow = lax.broadcasted_iota(jnp.int32, (HEAD, nkey), 0)
    vrows = jnp.where(nrow < 2, 1.0, 0.0).astype(bf16)
    valid = place_in[...] < lengths[0]
    augk = jnp.where(
        nrow == 0, jnp.where(valid, 0.0, -1e30), jnp.where(nrow < 4, 1.0, 0.0)
    ).astype(bf16)
    ga = ga_in[...].reshape(1, width)
    gm = gm_in[...].reshape(1, width)
    cos_t, sin_t = turn.at[0], turn.at[1]
    for pr in range(hc):
        kt[pr, 0, HEAD:, :] = augk
        kt[pr, 1, :HEAD, :] = augk
        vt[pr, 0, HEAD:, :] = vrows
        vt[pr, 1, :HEAD, :] = vrows
    gbuf[...] = jnp.zeros_like(gbuf)

    lane = lax.broadcasted_iota(jnp.int32, (tq, 2 * HEAD), 1)
    low_half = lane < HEAD

    def rotate(u, cs, sn, sign):
        half = HEAD // 2
        a, b = u[:half], u[half:]
        return jnp.concatenate([a * cs - sign * (b * sn), b * cs + sign * (a * sn)], axis=0)

    def kvcopies(i):
        cps = []
        cols = pl.ds(pl.multiple_of(c * ntok + i * tq, tq), tq)
        n = 0
        for ref in (kt, vt):
            for par in range(2):
                part = ref.at[:, par, pl.ds(par * HEAD, HEAD), cols]
                cps.append(remote(part, part, kss.at[i, n], krs.at[i, n], core))
                n += 1
        return cps

    for cp in locals_[NCH : NCH + 4]:
        cp.wait()
    for w in w_q:
        w.wait_recv()

    def qkv(i, carry):
        pltpu.make_async_copy(tok.at[pl.ds(i * cl, cl)], xall.at[i, x], lsem.at[i]).wait()
        xcopy(i).wait_recv()
        xb = xall[i].reshape(tq, width)
        here = pl.ds(pl.multiple_of(i * tq, tq), tq)
        cols = pl.ds(pl.multiple_of(c * ntok + i * tq, tq), tq)
        cs = cos_t[:, here]
        sn = sin_t[:, here]
        for cc in range(2):
            pt = dot(wqt[cc].reshape(3 * qw, width), xb, 1, 1)
            at = slice(cc * HEAD, cc * HEAD + HEAD)
            for j in range(hc):
                u = pt[j * 3 * HEAD : (j + 1) * 3 * HEAD]
                q = rotate(u[:HEAD], cs, sn, 1.0).astype(bf16)
                qt[cc, j, :, here] = (q.astype(f32) * 0.125).astype(bf16)
                kt[j, cc, at, cols] = rotate(u[HEAD : 2 * HEAD], cs, sn, 1.0).astype(bf16)
                vt[j, cc, at, cols] = u[2 * HEAD :].astype(bf16)
        for cp in kvcopies(i):
            cp.start()
        for j in range(hc):
            both = jnp.concatenate([qt[0, j, :, here], qt[1, j, :, here]], axis=0)
            nat = both.astype(f32).T
            qn[0, j, here, :] = jnp.where(
                low_half, nat, jnp.where(lane == HEAD, 1.0, 0.0)
            ).astype(bf16)
            qn[1, j, here, :] = jnp.where(
                low_half, jnp.where(lane == 0, 1.0, 0.0), nat
            ).astype(bf16)
        return carry

    lax.fori_loop(0, NCH, qkv, 0)

    def kvwait(i, carry):
        for cp in kvcopies(i):
            cp.wait_recv()
        return carry

    lax.fori_loop(0, NCH, kvwait, 0)
    w_ox.wait_recv()
    w_oxc.start()
    for cp in locals_[NCH + 4 :]:
        cp.wait()
    for w in (w_o, w_oxc, w_g, w_u, w_d):
        w.wait_recv()

    def rows_of(i):
        return pl.ds(pl.multiple_of(i * tq, tq), tq)

    def hid_rows(cc, i):
        return pl.ds(pl.multiple_of(cc * ntok + i * tq, tq), tq)

    def own_of(i):
        return pl.ds(pl.multiple_of(i * cl, cl), cl)

    def ocopy(i):
        part = oall.at[x, rows_of(i)]
        return remote(part, part, oss.at[i], ors.at[i], xp)

    def mcopy(i):
        return remote(snd1.at[i], mrecv.at[i], mss.at[i], mrs.at[i], xp)

    def bcopy(i):
        return remote(dmb.at[i, x], dmb.at[i, x], bss.at[i], brs.at[i], xp)

    def dcopy(i):
        return remote(snd2.at[i], drecv.at[i], dss.at[i], drs.at[i], xp)

    def acopy(i):
        return remote(dab.at[i, x], dab.at[i, x], ass_.at[i], ars.at[i], xp)

    def ycopy(i):
        return pltpu.make_async_copy(ybuf.at[i], out_y.at[own_of(i)], ysem.at[i])

    def attend(i):
        rows = rows_of(i)
        for j in range(hc):
            outs = []
            for par in range(2):
                base = HEAD * (1 - par)
                qq = qn[par, j, rows, :]
                s = dot(qq, kt[j, par])
                top = jnp.max(s, axis=1, keepdims=True)
                p = jnp.exp(s - top).astype(bf16)
                oo = dot(p, vt[j, par], 1, 1)
                total = oo[:, base : base + 1]
                outs.append(oo * (1.0 / total))
                neg = -(top + jnp.log(total))
                hi = neg.astype(bf16).astype(f32)
                mid = (neg - hi).astype(bf16).astype(f32)
                lo = neg - hi - mid
                qf = qq.astype(f32)
                qf = jnp.where(lane == base + 1, hi, qf)
                qf = jnp.where(lane == base + 2, mid, qf)
                qf = jnp.where(lane == base + 3, lo, qf)
                qn[par, j, rows, :] = qf.astype(bf16)
            oall[x, rows, j * 2 * HEAD : (j + 1) * 2 * HEAD] = jnp.where(
                low_half, outs[0], outs[1]
            ).astype(bf16)
        ocopy(i).start()

    def mlp_fwd(i):
        rows, own = rows_of(i), own_of(i)
        ocopy(i).wait_recv()
        a = dot(oall[0, rows, :], wo[0].reshape(2 * qw, width))
        a += dot(oall[1, rows, :], wo[1].reshape(2 * qw, width))
        r = xall[i].reshape(tq, width).astype(f32) + a
        centre = r - mean(r)
        inv = lax.rsqrt(mean(centre * centre) + eps)
        n1 = centre * inv
        tmp[...] = n1.reshape(2, cl, width)
        n1own[own, :] = tmp[x]
        itmp[...] = jnp.broadcast_to(inv, (tq, 128)).reshape(2, cl, 128)
        inv1own[own, :] = itmp[x]
        x1 = n1 * ga
        xb = x1.astype(bf16)
        x1b[rows, :] = xb
        m = None
        for cc in range(2):
            g = dot(xb, wm[3 * cc])
            u = dot(xb, wm[3 * cc + 1])
            sg = 0.5 * jnp.tanh(0.5 * g) + 0.5
            si = g * sg
            hv = (si * u).astype(bf16)
            at = hid_rows(cc, i)
            act2[at, :] = si.astype(bf16)
            act1[at, :] = (u * (sg + si * (1.0 - sg))).astype(bf16)
            hid[at, :] = hv
            part = dot(hv, wm[3 * cc + 2])
            m = part if m is None else m + part
        tmp[...] = m.reshape(2, cl, width)
        snd1[i] = tmp[ox].astype(bf16)
        mcopy(i).start()
        tmp[...] = (x1 + m).reshape(2, cl, width)
        rown[own, :] = tmp[x]

    def norm_two(i):
        own = own_of(i)
        mcopy(i).wait_recv()
        r = rown[own, :] + mrecv[i].astype(f32)
        centre = r - mean(r)
        inv = lax.rsqrt(mean(centre * centre) + eps)
        n2 = centre * inv
        ybuf[i] = (n2 * gm).astype(bf16)
        ycopy(i).start()
        dy = cotv[own, :].astype(f32)
        gbuf[1:2, :] += jnp.sum(dy * n2, axis=0, keepdims=True)
        e = dy * gm
        dr = inv * (e - mean(e) - n2 * mean(e * n2))
        rown[own, :] = dr
        dmb[i, x] = dr.astype(bf16)
        bcopy(i).start()

    def mlp_bwd(i):
        bcopy(i).wait_recv()
        db = dmb[i].reshape(tq, width)
        d = None
        for cc in range(2):
            at = hid_rows(cc, i)
            dh = dot(db, wm[3 * cc + 2], 1, 1)
            dg = (dh * act1[at, :].astype(f32)).astype(bf16)
            du = (dh * act2[at, :].astype(f32)).astype(bf16)
            act1[at, :] = dg
            act2[at, :] = du
            part = dot(dg, wm[3 * cc], 1, 1) + dot(du, wm[3 * cc + 1], 1, 1)
            d = part if d is None else d + part
        tmp[...] = d.reshape(2, cl, width)
        snd2[i] = tmp[ox].astype(bf16)
        own = own_of(i)
        rown[own, :] = rown[own, :] + tmp[x]

    def norm_one(i):
        own = own_of(i)
        dcopy(i).wait_recv()
        dx = rown[own, :] + drecv[i].astype(f32)
        n1 = n1own[own, :]
        gbuf[0:1, :] += jnp.sum(dx * n1, axis=0, keepdims=True)
        e = dx * ga
        dr = inv1own[own, 0:1] * (e - mean(e) - n1 * mean(e * n1))
        rown[own, :] = dr
        dab[i, x] = dr.astype(bf16)
        acopy(i).start()

    kb = min(1024, nkey)

    def attend_back(j, i):
        rows = rows_of(i)

        @when(j == 0)
        def _():
            acopy(i).wait_recv()

        @when(i == 0)
        def _():
            dkv[j % 2] = jnp.zeros(dkv.shape[1:], f32)

        da = dab[i].reshape(tq, width)
        cs = cos_t[:, rows]
        sn = sin_t[:, rows]
        lanes = pl.ds(pl.multiple_of(j * 2 * HEAD, 2 * HEAD), 2 * HEAD)
        dop = dot(da, wo[x, j].reshape(2 * HEAD, width), 1, 1).astype(bf16)
        dof = dop.astype(f32)
        prod = dof * oall[x, rows, lanes].astype(f32)
        dot_t = dof.T.astype(bf16)
        dqs = []
        for par in range(2):
            base = HEAD * (1 - par)
            mine = low_half if par == 0 else jnp.logical_not(low_half)
            neg = -jnp.sum(jnp.where(mine, prod, 0.0), axis=1, keepdims=True)
            hi = neg.astype(bf16).astype(f32)
            lo = neg - hi
            aug = jnp.where(lane == base, hi, jnp.where(lane == base + 1, lo, 0.0))
            doa = jnp.where(mine, dof, aug).astype(bf16)
            qq = qn[par, j, rows, :]
            dq = None
            for b in range(nkey // kb):
                kk = slice(b * kb, (b + 1) * kb)
                p = jnp.exp(dot(qq, kt[j, par, :, kk]))
                d = dot(doa, vt[j, par, :, kk])
                ds = (p * d).astype(bf16)
                pb = p.astype(bf16)
                dkv[j % 2, par, HEAD:, kk] += dot(dot_t[par * HEAD : (par + 1) * HEAD], pb)
                dkv[j % 2, par, :HEAD, kk] += dot(qt[par, j, :, rows], ds)
                part = dot(ds, kt[j, par, :, kk], 1, 1)
                dq = part if dq is None else dq + part
            dqs.append(dq)
        dqt = jnp.where(low_half, dqs[0], dqs[1]).T * 0.125
        at = pl.ds(pl.multiple_of(j * 3 * HEAD, HEAD), HEAD)
        for par in range(2):
            u = rotate(dqt[par * HEAD : (par + 1) * HEAD], cs, sn, -1.0)
            dpt[par, at, rows] = u.astype(bf16)

    g_own = (0, 1, 6)
    g_got = (3, 4, 7)
    g_sent = (2, 5, 8)

    def gcopy(n):
        return remote(wm.at[g_sent[n]], wm.at[g_got[n]], gss.at[n], grs.at[n], core)

    def give(n, dev):
        pl.semaphore_signal(credit.at[n], inc=1, device_id=dev, device_id_type=MESH)

    def tall(ref, cc):
        return ref.at[pl.ds(pl.multiple_of(cc * ntok, ntok), ntok)]

    def grad_into(dst, left, right):
        tile = min(256, width)

        def one(n, carry):
            at = pl.ds(pl.multiple_of(n * tile, tile), tile)
            dst[at, :] = dot(left[:, at], right[...].reshape(ntok, width), 0, 0).astype(bf16)
            return carry

        lax.fori_loop(0, width // tile, one, 0)

    def grad(n):
        left = (x1b, x1b, hid)[n]
        right = (act1, act2, dmb)[n]
        if n < 2:
            grad_into(wm.at[g_sent[n]], left, tall(right, oc))
            grad_into(wm.at[g_own[n]], left, tall(right, c))
            if n == 0:
                pl.semaphore_wait(credit.at[0], 1)
            gcopy(n).start()
        else:
            grad_into(wm.at[g_sent[n]], tall(left, oc), right)
            gcopy(n).start()
            grad_into(wm.at[g_own[n]], tall(left, c), right)
        if n == 2 and ring:
            give(2, zdev)

            @when(outer)
            def _():
                give(2, ydev)

            @when(inner)
            def _():
                give(2, mid)

        if n == 1:
            give(1, core)

            def sent(i, carry):
                bcopy(i).wait_send()
                return carry

            lax.fori_loop(0, NCH, sent, 0)
            if ring:
                give(3, ydev)
                give(3, zdev)

                @when(inner)
                def _():
                    give(3, mid)

    def gsum(n):
        gcopy(n).wait()
        own, got = g_own[n], g_got[n]
        wm[own] = (wm[own].astype(f32) + wm[got].astype(f32)).astype(bf16)
        if n == 2 and ring:
            pl.semaphore_wait(credit.at[2], 2)

    def weights_free():
        give(0, core)

    def buffers_free():
        pl.semaphore_wait(credit.at[1], 1)
        if ring:
            pl.semaphore_wait(credit.at[3], 2 + jnp.where(inner, 1, 0))

    place = jnp.where(y == 0, z, 7 - z)
    seg = fq // 16
    hops = 14

    def ring_row(p):
        p = (p + 8) % 8
        return {"rows": jnp.where(p < 4, 2 * p, 15 - 2 * p)}

    def ring_copies(u, k, to_slot):
        cps = []
        for d in range(2):
            sign = 1 - 2 * d
            at = d * 8 * seg + ((place - sign * k + 16) % 8) * seg
            rows = pl.ds(pl.multiple_of(at, 16), seg)
            if to_slot:
                slot = ((u * 2 + d) * 7 + k) * seg
                part = wm.at[ring_own(u), rows]
                dst = hid.at[pl.ds(pl.multiple_of(slot, 16), seg)]
            else:
                part = dst = wm.at[ring_final(u), rows]
            cps.append(
                remote(part, dst, rss.at[u, d, k], rrs.at[u, d, k], ring_row(place + sign))
            )
        return cps

    def ring_own(u):
        return jnp.where(u == 0, 6, u - 1)

    def ring_final(u):
        return jnp.where(u == 0, 7, u + 2)

    def ring_step(m):
        u = m % 3
        k = m // 3 - RING_LAG * u
        live = jnp.logical_and(k >= 0, k <= hops)

        @when(jnp.logical_and(live, k >= 1))
        def _():
            for cp in ring_copies(u, k - 1, False):
                cp.wait_recv()

        @when(jnp.logical_and(k >= 1, k <= 7))
        def _():
            for d in range(2):
                sign = 1 - 2 * d
                at = d * 8 * seg + ((place - sign * k + 16) % 8) * seg
                rows = pl.ds(pl.multiple_of(at, 16), seg)
                slot = pl.ds(pl.multiple_of(((u * 2 + d) * 7 + k - 1) * seg, 16), seg)
                src = ring_own(u)
                wm[jnp.where(k == 7, ring_final(u), src), rows, :] = (
                    wm[src, rows, :].astype(f32) + hid[slot, :].astype(f32)
                ).astype(bf16)

        @when(jnp.logical_and(live, k <= 6))
        def _():
            for cp in ring_copies(u, k, True):
                cp.start()

        @when(jnp.logical_and(k >= 7, k < hops))
        def _():
            for cp in ring_copies(u, k, False):
                cp.start()

        @when(jnp.logical_and(live, k >= 2))
        def _():
            for cp in ring_copies(u, k - 2, False):
                cp.wait_send()

    sub = 3 * HEAD

    def acore(b):
        src = act2.at[pl.ds(pl.multiple_of((4 + b) * sub, sub), sub)]
        dst = act2.at[pl.ds(pl.multiple_of(b * sub, sub), sub)]
        return remote(src, dst, gss.at[3 + b], grs.at[3 + b], core)

    def asum(b):
        acore(b).wait()
        got = act2[pl.ds(pl.multiple_of(b * sub, sub), sub), :]
        rows = pl.ds(pl.multiple_of(b * sub, sub), sub)
        agrad[rows, :] = (agrad[rows, :].astype(f32) + got.astype(f32)).astype(bf16)

    def astart(b, theirs, ours):
        act2[pl.ds(pl.multiple_of((4 + b) * sub, sub), sub), :] = theirs.astype(bf16)
        acore(b).start()
        agrad[pl.ds(pl.multiple_of(b * sub, sub), sub), :] = ours.astype(bf16)

    hs = sub // 2

    def tree(b, phase):
        mine = agrad.at[pl.ds(pl.multiple_of(b * sub + y * hs, hs), hs)]
        final = act2.at[pl.ds(pl.multiple_of(b * sub + y * hs, hs), hs)]
        buf_a = x1b.at[pl.ds(pl.multiple_of(b * sub, hs), hs)]
        buf_b = x1b.at[pl.ds(pl.multiple_of(b * sub + hs, hs), hs)]
        buf_c = dmb.at[b, 0, pl.ds(0, hs)]
        c0 = lambda: remote(agrad.at[pl.ds(pl.multiple_of(b * sub + (1 - y) * hs, hs), hs)], buf_a, fas.at[b, 0], far.at[b, 0], ydev)
        c1 = lambda: remote(mine, buf_b, fas.at[b, 1], far.at[b, 1], zdev)
        c2 = lambda: remote(mine, buf_c, fas.at[b, 2], far.at[b, 2], mid)
        c3 = lambda: remote(final, final, fas.at[b, 3], far.at[b, 3], zdev)
        c4 = lambda: remote(final, final, fas.at[b, 4], far.at[b, 4], ydev)

        def add(buf, dst):
            dst[...] = (mine[...].astype(f32) + buf[...].astype(f32)).astype(bf16)

        if phase == 0:
            c0().start()
        elif phase == 1:
            c0().wait_recv()
            add(buf_a, mine)

            @when(outer)
            def _():
                c1().start()
        elif phase == 2:

            @when(inner)
            def _():
                c1().wait_recv()
                add(buf_b, mine)
                c2().start()
        elif phase == 3:

            @when(inner)
            def _():
                c2().wait()
                add(buf_c, final)
                c3().start()
                c4().start()
        elif phase == 4:

            @when(outer)
            def _():
                c3().wait_recv()
                c4().start()
        else:
            c4().wait_recv()
            c0().wait_send()
            c4().wait_send()

            @when(outer)
            def _():
                c1().wait_send()

            @when(inner)
            def _():
                c3().wait_send()

    def gain_copy(n):
        return remote(gbuf, grecv.at[n], ns.at[n], nr.at[n], doubling[n])

    def gain_step(n):
        if n > 0:
            gain_copy(n - 1).wait()
            gbuf[...] += grecv[n - 1]
        if n < len(doubling):
            gain_copy(n).start()

    theirs_cols = pl.ds(pl.multiple_of(oc * ntok, ntok), ntok)
    mine_cols = pl.ds(pl.multiple_of(c * ntok, ntok), ntok)

    def kv_rows(j):
        return pl.ds(pl.multiple_of(j * 3 * HEAD + HEAD, HEAD), 2 * HEAD)

    def kvback(j):
        return remote(dpt.at[:, kv_rows(j)], dkvr.at[j], css.at[j], crs.at[j], core)

    def kv_send(j):
        dpt[:, kv_rows(j), :] = dkv[j % 2, :, :, theirs_cols].astype(bf16)
        kvback(j).start()

    def kv_finish(j):
        kvback(j).wait()
        base = j * 3 * HEAD
        for par in range(2):
            u = dkv[j % 2, par, :, mine_cols] + dkvr[j, par].astype(f32)
            dk = rotate(u[:HEAD], cos_t[...], sin_t[...], -1.0)
            dpt[par, pl.ds(pl.multiple_of(base + HEAD, HEAD), HEAD), :] = dk.astype(bf16)
            dpt[par, pl.ds(pl.multiple_of(base + 2 * HEAD, HEAD), HEAD), :] = u[HEAD:].astype(bf16)

    def qkv_grads(j):
        rows = pl.ds(pl.multiple_of(j * sub, HEAD), sub)
        xr = xall[...].reshape(ntok, width)
        astart(1 + j, dot(dpt[oc, rows, :], xr), dot(dpt[c, rows, :], xr))

    def out_grads():
        both = dot(oall[x], dab[...].reshape(ntok, width), 0, 0).reshape(hc, 2, HEAD, width)
        first = both[:, 0].reshape(sub, width)
        second = both[:, 1].reshape(sub, width)
        astart(0, jnp.where(c == 0, second, first), jnp.where(c == 0, first, second))

    def fcopy(i):
        return remote(snd1.at[i], mrecv.at[i], fss.at[i], frs.at[i], xp)

    def input_terms(i, who):
        cols = pl.ds(pl.multiple_of(i * tq + who * cl, cl), cl)
        d = None
        for cc in range(2):
            part = dot(dpt[cc, :, cols], wqt[cc].reshape(3 * qw, width), 0, 0)
            d = part if d is None else d + part
        return d

    def input_send(i):
        mcopy(i).wait_send()
        snd1[i] = input_terms(i, ox).astype(bf16)
        fcopy(i).start()

    def dxcopy(i):
        return pltpu.make_async_copy(ybuf.at[i], out_dx.at[own_of(i)], lsem.at[i])

    def input_finish(i):
        d = input_terms(i, x)
        fcopy(i).wait_recv()
        d = rown[own_of(i), :] + (d + mrecv[i].astype(f32))
        ycopy(i).wait()
        ybuf[i] = d.astype(bf16)
        dxcopy(i).start()

    def kv_done(j):
        kv_finish(j)
        qkv_grads(j)

    handlers = {
        "S0": attend,
        "S1": mlp_fwd,
        "S2": norm_two,
        "S3": mlp_bwd,
        "D": lambda i: dcopy(i).start(),
        "S4": norm_one,
        "S5": lambda q: attend_back(q // NCH, q % NCH),
        "kvs": kv_send,
        "kvf": kv_done,
        "og": lambda i: out_grads(),
        "as": asum,
        "C0": lambda i: weights_free(),
        "C1": lambda i: buffers_free(),
        "I": input_send,
        "F": input_finish,
    }
    for n in range(3):
        handlers["G%d" % n] = functools.partial(lambda n, i: grad(n), n)
        handlers["gs%d" % n] = functools.partial(lambda n, i: gsum(n), n)
    for n in range(len(doubling) + 1):
        handlers["N%d" % n] = functools.partial(lambda n, i: gain_step(n), n)
    if ring:
        for ph in range(6):
            handlers["T%d" % ph] = functools.partial(lambda ph, b: tree(b, ph), ph)

    plan = [(kind, arg) for kind, arg in make_plan(len(doubling)) if kind in handlers or kind == "R"]
    big = []
    count = 0
    for kind, arg in plan:
        if kind == "R":
            count += arg
            big[-1][2] = count
        else:
            big.append([kind, arg, count])

    total_ring = 3 * (hops + 1 + 2 * RING_LAG)
    big[-1][2] = total_ring
    kinds = sorted({b[0] for b in big}, key=[b[0] for b in big].index)

    packed = [
        kinds.index(kind) + 64 * (arg + 16 * min(ends, total_ring)) for kind, arg, ends in big
    ]

    def entry(t):
        value = packed[0]
        for n in range(1, len(packed)):
            value = jnp.where(t >= n, packed[n], value)
        return value % 64, (value // 64) % 16, value // 1024

    def dispatch(code, arg, first, last):
        if last - first == 1:
            handlers[kinds[first]](arg)
            return
        middle = (first + last) // 2

        @when(code < middle)
        def _():
            dispatch(code, arg, first, middle)

        @when(code >= middle)
        def _():
            dispatch(code, arg, middle, last)

    def one_step(t, done):
        code, arg, ends = entry(t)
        dispatch(code, arg, 0, len(kinds))
        if not ring:
            return done

        def ring_one(m, carry):
            ring_step(m)
            return carry

        lax.fori_loop(done, ends, ring_one, 0)
        return ends

    lax.fori_loop(0, len(big), one_step, 0)

    def result_copies():
        first, third = (3, 7) if ring else (0, 6)
        att = act2 if ring else agrad
        cps = [
            pltpu.make_async_copy(wm.at[pl.ds(first, 2)], g_mlp.at[pl.ds(0, 2)], gls.at[0]),
            pltpu.make_async_copy(wm.at[third], g_mlp.at[2], gls.at[1]),
            pltpu.make_async_copy(att.at[pl.ds(0, sub)], g_out, gls.at[2]),
        ]
        for j in range(hc):
            for n in range(3):
                rows = pl.ds((1 + j) * sub + n * HEAD, HEAD)
                cps.append(
                    pltpu.make_async_copy(att.at[rows], g_qkv.at[n, j], gls.at[len(cps)])
                )
        return cps

    for cp in result_copies():
        cp.start()
    g_ga[...] = gbuf[0:1, :]
    g_gm[...] = gbuf[1:2, :]

    for i in range(NCH):
        dxcopy(i).wait()
        xcopy(i).wait_send()
        for cp in kvcopies(i):
            cp.wait_send()
        ocopy(i).wait_send()
        dcopy(i).wait_send()
        acopy(i).wait_send()
        fcopy(i).wait_send()
    for w in (*w_q, w_o, w_ox, w_oxc, w_g, w_u, w_d):
        w.wait_send()
    if ring:
        for u in range(3):
            for cp in ring_copies(u, hops - 1, False):
                cp.wait_send()
    for cp in result_copies():
        cp.wait()


RING_LAG = 2


def make_plan(doublings):
    plan = [
        ("S0", 0), ("S0", 1), ("S0", 2), ("S0", 3), ("S1", 0), ("S1", 1), ("S1", 2), ("S2", 0),
        ("S1", 3), ("S2", 1), ("S2", 2), ("S3", 0), ("S2", 3), ("D", 0), ("S3", 1), ("D", 1),
        ("S3", 2), ("D", 2), ("S3", 3), ("C0", 0), ("D", 3), ("G2", 0), ("S4", 0), ("G0", 0),
        ("gs2", 0), ("R", 3), ("S4", 1), ("S4", 2), ("G1", 0), ("R", 3), ("gs0", 0), ("S4", 3),
        ("S5", 0), ("N0", 0), ("R", 3), ("gs1", 0), ("C1", 0), ("S5", 4), ("N1", 0), ("R", 1),
        ("S5", 1), ("N2", 0), ("R", 3), ("S5", 2), ("N3", 0), ("R", 2), ("S5", 3), ("N4", 0),
        ("R", 2), ("og", 0), ("R", 1), ("kvs", 0), ("S5", 5), ("N5", 0), ("R", 2), ("kvf", 0),
        ("R", 1), ("as", 0), ("T0", 0), ("S5", 6), ("R", 3), ("as", 1), ("T0", 1), ("S5", 7),
        ("T1", 0), ("kvs", 1), ("S5", 8), ("R", 3), ("kvf", 1), ("T2", 0), ("S5", 9), ("T1", 1),
        ("R", 1), ("as", 2), ("T0", 2), ("S5", 10), ("T3", 0), ("R", 2), ("T2", 1), ("S5", 11),
        ("T1", 2), ("R", 1), ("kvs", 2), ("T4", 0), ("R", 2), ("kvf", 2), ("T3", 1), ("T2", 2),
        ("I", 0), ("I", 1), ("I", 2), ("R", 1), ("as", 3), ("T0", 3), ("T5", 0), ("I", 3),
        ("R", 2), ("T4", 1), ("F", 0), ("T3", 2), ("R", 1), ("T1", 3), ("R", 2), ("T4", 2),
        ("T5", 1), ("R", 1), ("T2", 3), ("R", 2), ("F", 1), ("F", 2), ("F", 3), ("T3", 3),
        ("T5", 2), ("R", 1), ("T4", 3), ("R", 3), ("T5", 3), ("R", 11),
    ]
    return plan + [("N%d" % n, 0) for n in range(6, doublings + 1)]


def on_device(
    nrows, tokens, lengths, w_qkv, w_out, w_gate, w_up, w_down, gain_attn, gain_mlp, cotangent
):
    _, length, width = tokens.shape
    qw = w_qkv.shape[2]
    fq = w_gate.shape[1]
    hc = qw // HEAD
    nh = 2 * hc
    cl = length // NCH
    tq = 2 * cl
    ntok = 2 * length
    nkey = 2 * ntok
    cores, chunk, xs, place = np.meshgrid(
        np.arange(2), np.arange(NCH), np.arange(2), np.arange(cl), indexing="ij"
    )
    position = ((2 * xs + cores) * length + chunk * cl + place).reshape(2, ntok)
    half = HEAD // 2
    freqs = rope_base ** (-np.arange(half) / half)
    angles = freqs[None, :, None] * position[:, None, :]
    turns = np.stack([np.cos(angles), np.sin(angles)], axis=1).astype(np.float32)
    places = position.reshape(1, nkey).astype(np.int32)

    hbm = pl.BlockSpec(memory_space=pl.ANY)
    vmem = pl.BlockSpec(memory_space=pltpu.VMEM)
    S = jax.ShapeDtypeStruct
    V = pltpu.VMEM
    dma = pltpu.SemaphoreType.DMA
    doublings = 2 + (nrows - 1).bit_length()
    scratch = [
        V((NCH, 2, cl, width), bf16),
        V((length, width), bf16),
        V((2, hc, 3, HEAD, width), bf16),
        V((2, hc, 2, HEAD, width), bf16),
        V((9, width, fq), bf16),
        V((hc, 2, 2 * HEAD, nkey), bf16),
        V((hc, 2, 2 * HEAD, nkey), bf16),
        V((2, hc, ntok, 2 * HEAD), bf16),
        V((2, hc, HEAD, ntok), bf16),
        V((2, ntok, 2 * qw), bf16),
        V((ntok, width), bf16),
        V((length, width), f32),
        V((length, width), f32),
        V((length, 128), f32),
        V((2 * ntok, fq), bf16),
        V((2 * ntok, fq), bf16),
        V((2 * ntok, fq), bf16),
        V((NCH, 2, cl, width), bf16),
        V((NCH, 2, cl, width), bf16),
        V((NCH, cl, width), bf16),
        V((NCH, cl, width), bf16),
        V((NCH, cl, width), bf16),
        V((NCH, cl, width), bf16),
        V((2, cl, width), f32),
        V((2, cl, 128), f32),
        V((2, 2, 2 * HEAD, nkey), f32),
        V((hc, 2, 2 * HEAD, ntok), bf16),
        V((2, 3 * qw, ntok), bf16),
        V((NCH, cl, width), bf16),
        V(((1 + hc) * 3 * HEAD, width), bf16),
        V((8, width), f32),
        V((doublings, 8, width), f32),
        V((2, HEAD // 2, ntok), f32),
        dma((NCH + 9,)),
        dma((3,)), dma((3,)),
        dma((7,)), dma((7,)),
        dma((NCH,)), dma((NCH,)),
        dma((NCH, 4)), dma((NCH, 4)),
        dma((NCH,)), dma((NCH,)),
        dma((NCH,)), dma((NCH,)),
        dma((NCH,)), dma((NCH,)),
        dma((NCH,)), dma((NCH,)),
        dma((NCH,)), dma((NCH,)),
        dma((hc,)), dma((hc,)),
        dma((NCH,)), dma((NCH,)),
        dma((4 + hc,)), dma((4 + hc,)), dma((3 + 3 * hc,)),
        dma((3, 2, 14)), dma((3, 2, 14)),
        dma((1 + hc, 5)), dma((1 + hc, 5)),
        dma((doublings,)), dma((doublings,)),
        dma((NCH,)),
        pltpu.SemaphoreType.REGULAR((4,)),
    ]
    outs = pl.pallas_call(
        functools.partial(layer_kernel, nrows),
        out_shape=[
            S((length, width), bf16), S((length, width), bf16),
            S((3, width, fq), bf16), S((qw, width), bf16), S((3, hc, HEAD, width), bf16),
            S((1, width), f32), S((1, width), f32),
        ],
        in_specs=[hbm] * 8 + [pl.BlockSpec(memory_space=pltpu.SMEM)] + [vmem] * 3,
        out_specs=[hbm] * 5 + [vmem] * 2,
        scratch_shapes=scratch,
        compiler_params=pltpu.CompilerParams(
            collective_id=0, has_side_effects=True, vmem_limit_bytes=VLIM
        ),
    )(
        tokens[0], cotangent[0],
        w_qkv.transpose(0, 2, 1).reshape(3, hc, HEAD, width), w_out.reshape(hc, HEAD, width), w_gate, w_up, w_down,
        jnp.asarray(turns), lengths, gain_attn, gain_mlp, jnp.asarray(places),
    )
    y, dx, g_mlp, g_out, g_qkv, g_ga, g_gm = outs
    if nrows != 8:
        g_mlp, g_out, g_qkv = lax.psum((g_mlp, g_out, g_qkv), "rows")
    return (
        y[None], dx[None], g_qkv.astype(f32).reshape(3, qw, width).transpose(0, 2, 1),
        g_out.astype(f32), g_mlp[0].astype(f32), g_mlp[1].astype(f32), g_mlp[2].astype(f32),
        g_ga[0], g_gm[0],
    )


VLIM = 64 * 2**20


def solution(mesh):
    in_specs = (
        P("rows", "heads", None),
        P("rows"),
        P(None, None, "heads"),
        P("heads", None),
        P(None, "heads"),
        P(None, "heads"),
        P("heads", None),
        P(),
        P(),
        P("rows", "heads", None),
    )
    out_specs = (
        P("rows", "heads", None),
        P("rows", "heads", None),
        P(None, None, "heads"),
        P("heads", None),
        P(None, "heads"),
        P(None, "heads"),
        P("heads", None),
        P(),
        P(),
    )
    return jax.shard_map(
        functools.partial(on_device, mesh.shape["rows"]), mesh=mesh, in_specs=in_specs, out_specs=out_specs, check_vma=False
    )
```

```python
import functools

import jax
import jax.numpy as jnp
import numpy as np
from jax import lax
from jax.experimental import pallas as pl
from jax.experimental.pallas import tpu as pltpu
from jax.sharding import PartitionSpec as P

HEAD = 64
eps = 1e-05
rope_base = 1000.0
MESH = pl.DeviceIdType.MESH
f32 = jnp.float32
bf16 = jnp.bfloat16
NCH = 4


def dot(a, b, ca=1, cb=0):
    return lax.dot_general(a, b, (((ca,), (cb,)), ((), ())), preferred_element_type=f32)


def mean(a):
    return jnp.mean(a, axis=-1, keepdims=True)


def layer_kernel(
    nrows, tok, cot, wq_in, wo_in, wg_in, wu_in, wd_in, turns, lengths, ga_in, gm_in, place_in,
    out_y, out_dx, g_mlp, g_out, g_qkv, g_ga, g_gm,
    xall, cotv, wqt, wo, wm, kt, vt, qn, qt, oall, x1b, rown, n1own, inv1own,
    act1, act2, hid, dmb, dab, mrecv, drecv, snd1, snd2, tmp, itmp,
    dkv, dkvr, dpt, ybuf, agrad, gbuf, grecv, turn,
    lsem, wqs, wqr, wss, wrs, xss, xrs, kss, krs, oss, ors, mss, mrs, bss, brs, dss, drs, ass_, ars,
    css, crs, fss, frs, gss, grs, gls, rss, rrs, fas, far, ns, nr, ysem, credit,
):
    ring = nrows == 8
    length, width = tok.shape
    cl = length // NCH
    tq = 2 * cl
    ntok = 2 * length
    nkey = 2 * ntok
    hc = wo_in.shape[0]
    qw = hc * HEAD
    fq = wg_in.shape[1]

    h = lax.axis_index("heads")
    r = lax.axis_index("rows")
    x = h // 2
    c = h % 2
    oc = 1 - c
    ox = 1 - x
    core = {"heads": h + 1 - 2 * c}
    xp = {"heads": h + 2 - 4 * x}
    y = r % 2
    z = r // 2
    outer = jnp.logical_or(z == 0, z == 3)
    inner = jnp.logical_not(outer)
    ydev = {"rows": r + 1 - 2 * y}
    zdev = {"rows": r + 2 - 4 * (z % 2)}
    mid = {"rows": (3 - z) * 2 + y}
    doubling = [core, xp]
    span = 1
    while span < nrows:
        doubling.append({"rows": r + span - 2 * span * ((r // span) % 2)})
        span *= 2

    def when(cond):
        return pl.when(cond)

    def remote(src, dst, ss, rs, dev):
        return pltpu.make_async_remote_copy(
            src_ref=src, dst_ref=dst, send_sem=ss, recv_sem=rs, device_id=dev, device_id_type=MESH
        )

    barrier = pltpu.get_barrier_semaphore()
    for dev in doubling:
        pl.semaphore_signal(barrier, inc=1, device_id=dev, device_id_type=MESH)
    greeted = len(doubling)
    if ring:

        @when(inner)
        def _():
            pl.semaphore_signal(barrier, inc=1, device_id=mid, device_id_type=MESH)

        greeted = greeted + jnp.where(inner, 1, 0)

    def local_copies():
        cps = []
        for i in range(NCH):
            cps.append(pltpu.make_async_copy(tok.at[pl.ds(i * cl, cl)], xall.at[i, x], lsem.at[i]))
        n = NCH
        for src, dst in (
            (wq_in.at[0], wqt.at[c, :, 0]), (wq_in.at[1], wqt.at[c, :, 1]),
            (wq_in.at[2], wqt.at[c, :, 2]), (turns.at[c], turn), (wo_in, wo.at[x, :, c]), (wg_in, wm.at[3 * c]),
            (wu_in, wm.at[3 * c + 1]), (wd_in, wm.at[3 * c + 2]), (cot, cotv),
        ):
            cps.append(pltpu.make_async_copy(src, dst, lsem.at[n]))
            n += 1
        return cps

    locals_ = local_copies()
    for cp in locals_:
        cp.start()

    pl.semaphore_wait(barrier, greeted)

    def xcopy(i):
        return remote(tok.at[pl.ds(i * cl, cl)], xall.at[i, x], xss.at[i], xrs.at[i], xp)

    w_q = [
        remote(wq_in.at[n], wqt.at[c, :, n], wqs.at[n], wqr.at[n], core) for n in range(3)
    ]
    w_o = remote(wo_in, wo.at[x, :, c], wss.at[1], wrs.at[1], core)
    w_ox = remote(wo_in, wo.at[x, :, c], wss.at[2], wrs.at[2], xp)
    w_oxc = remote(wo.at[ox, :, c], wo.at[ox, :, c], wss.at[3], wrs.at[3], core)
    w_g = remote(wg_in, wm.at[3 * c], wss.at[4], wrs.at[4], core)
    w_u = remote(wu_in, wm.at[3 * c + 1], wss.at[5], wrs.at[5], core)
    w_d = remote(wd_in, wm.at[3 * c + 2], wss.at[6], wrs.at[6], core)
    for w in w_q:
        w.start()
    for i in range(NCH):
        xcopy(i).start()
    w_o.start()
    w_g.start()
    w_u.start()
    w_d.start()
    w_ox.start()

    nrow = lax.broadcasted_iota(jnp.int32, (HEAD, nkey), 0)
    vrows = jnp.where(nrow < 2, 1.0, 0.0).astype(bf16)
    valid = place_in[...] < lengths[0]
    augk = jnp.where(
        nrow == 0, jnp.where(valid, 0.0, -1e30), jnp.where(nrow < 4, 1.0, 0.0)
    ).astype(bf16)
    ga = ga_in[...].reshape(1, width)
    gm = gm_in[...].reshape(1, width)
    cos_t, sin_t = turn.at[0], turn.at[1]
    for pr in range(hc):
        kt[pr, 0, HEAD:, :] = augk
        kt[pr, 1, :HEAD, :] = augk
        vt[pr, 0, HEAD:, :] = vrows
        vt[pr, 1, :HEAD, :] = vrows
    gbuf[...] = jnp.zeros_like(gbuf)

    lane = lax.broadcasted_iota(jnp.int32, (tq, 2 * HEAD), 1)
    low_half = lane < HEAD

    def rotate(u, cs, sn, sign):
        half = HEAD // 2
        a, b = u[:half], u[half:]
        return jnp.concatenate([a * cs - sign * (b * sn), b * cs + sign * (a * sn)], axis=0)

    def kvcopies(i):
        cps = []
        cols = pl.ds(pl.multiple_of(c * ntok + i * tq, tq), tq)
        n = 0
        for ref in (kt, vt):
            for par in range(2):
                part = ref.at[:, par, pl.ds(par * HEAD, HEAD), cols]
                cps.append(remote(part, part, kss.at[i, n], krs.at[i, n], core))
                n += 1
        return cps

    for cp in locals_[NCH : NCH + 4]:
        cp.wait()
    for w in w_q:
        w.wait_recv()

    def qkv(i, carry):
        pltpu.make_async_copy(tok.at[pl.ds(i * cl, cl)], xall.at[i, x], lsem.at[i]).wait()
        xcopy(i).wait_recv()
        xb = xall[i].reshape(tq, width)
        here = pl.ds(pl.multiple_of(i * tq, tq), tq)
        cols = pl.ds(pl.multiple_of(c * ntok + i * tq, tq), tq)
        cs = cos_t[:, here]
        sn = sin_t[:, here]
        for cc in range(2):
            pt = dot(wqt[cc].reshape(3 * qw, width), xb, 1, 1)
            at = slice(cc * HEAD, cc * HEAD + HEAD)
            for j in range(hc):
                u = pt[j * 3 * HEAD : (j + 1) * 3 * HEAD]
                q = rotate(u[:HEAD], cs, sn, 1.0).astype(bf16)
                qt[cc, j, :, here] = (q.astype(f32) * 0.125).astype(bf16)
                kt[j, cc, at, cols] = rotate(u[HEAD : 2 * HEAD], cs, sn, 1.0).astype(bf16)
                vt[j, cc, at, cols] = u[2 * HEAD :].astype(bf16)
        for cp in kvcopies(i):
            cp.start()
        for j in range(hc):
            both = jnp.concatenate([qt[0, j, :, here], qt[1, j, :, here]], axis=0)
            nat = both.astype(f32).T
            qn[0, j, here, :] = jnp.where(
                low_half, nat, jnp.where(lane == HEAD, 1.0, 0.0)
            ).astype(bf16)
            qn[1, j, here, :] = jnp.where(
                low_half, jnp.where(lane == 0, 1.0, 0.0), nat
            ).astype(bf16)
        return carry

    lax.fori_loop(0, NCH, qkv, 0)

    def kvwait(i, carry):
        for cp in kvcopies(i):
            cp.wait_recv()
        return carry

    lax.fori_loop(0, NCH, kvwait, 0)
    w_ox.wait_recv()
    w_oxc.start()
    for cp in locals_[NCH + 4 :]:
        cp.wait()
    for w in (w_o, w_oxc, w_g, w_u, w_d):
        w.wait_recv()

    def rows_of(i):
        return pl.ds(pl.multiple_of(i * tq, tq), tq)

    def hid_rows(cc, i):
        return pl.ds(pl.multiple_of(cc * ntok + i * tq, tq), tq)

    def own_of(i):
        return pl.ds(pl.multiple_of(i * cl, cl), cl)

    def ocopy(i):
        part = oall.at[x, rows_of(i)]
        return remote(part, part, oss.at[i], ors.at[i], xp)

    def mcopy(i):
        return remote(snd1.at[i], mrecv.at[i], mss.at[i], mrs.at[i], xp)

    def bcopy(i):
        return remote(dmb.at[i, x], dmb.at[i, x], bss.at[i], brs.at[i], xp)

    def dcopy(i):
        return remote(snd2.at[i], drecv.at[i], dss.at[i], drs.at[i], xp)

    def acopy(i):
        return remote(dab.at[i, x], dab.at[i, x], ass_.at[i], ars.at[i], xp)

    def ycopy(i):
        return pltpu.make_async_copy(ybuf.at[i], out_y.at[own_of(i)], ysem.at[i])

    def attend(i):
        rows = rows_of(i)
        for j in range(hc):
            outs = []
            for par in range(2):
                base = HEAD * (1 - par)
                qq = qn[par, j, rows, :]
                s = dot(qq, kt[j, par])
                top = jnp.max(s, axis=1, keepdims=True)
                p = jnp.exp(s - top).astype(bf16)
                oo = dot(p, vt[j, par], 1, 1)
                total = oo[:, base : base + 1]
                outs.append(oo * (1.0 / total))
                neg = -(top + jnp.log(total))
                hi = neg.astype(bf16).astype(f32)
                mid = (neg - hi).astype(bf16).astype(f32)
                lo = neg - hi - mid
                qf = qq.astype(f32)
                qf = jnp.where(lane == base + 1, hi, qf)
                qf = jnp.where(lane == base + 2, mid, qf)
                qf = jnp.where(lane == base + 3, lo, qf)
                qn[par, j, rows, :] = qf.astype(bf16)
            oall[x, rows, j * 2 * HEAD : (j + 1) * 2 * HEAD] = jnp.where(
                low_half, outs[0], outs[1]
            ).astype(bf16)
        ocopy(i).start()

    def mlp_fwd(i):
        rows, own = rows_of(i), own_of(i)
        ocopy(i).wait_recv()
        a = dot(oall[0, rows, :], wo[0].reshape(2 * qw, width))
        a += dot(oall[1, rows, :], wo[1].reshape(2 * qw, width))
        r = xall[i].reshape(tq, width).astype(f32) + a
        centre = r - mean(r)
        inv = lax.rsqrt(mean(centre * centre) + eps)
        n1 = centre * inv
        tmp[...] = n1.reshape(2, cl, width)
        n1own[own, :] = tmp[x]
        itmp[...] = jnp.broadcast_to(inv, (tq, 128)).reshape(2, cl, 128)
        inv1own[own, :] = itmp[x]
        x1 = n1 * ga
        xb = x1.astype(bf16)
        x1b[rows, :] = xb
        m = None
        for cc in range(2):
            g = dot(xb, wm[3 * cc])
            u = dot(xb, wm[3 * cc + 1])
            sg = 0.5 * jnp.tanh(0.5 * g) + 0.5
            si = g * sg
            hv = (si * u).astype(bf16)
            at = hid_rows(cc, i)
            act2[at, :] = si.astype(bf16)
            act1[at, :] = (u * (sg + si * (1.0 - sg))).astype(bf16)
            hid[at, :] = hv
            part = dot(hv, wm[3 * cc + 2])
            m = part if m is None else m + part
        tmp[...] = m.reshape(2, cl, width)
        snd1[i] = tmp[ox].astype(bf16)
        mcopy(i).start()
        tmp[...] = (x1 + m).reshape(2, cl, width)
        rown[own, :] = tmp[x]

    def norm_two(i):
        own = own_of(i)
        mcopy(i).wait_recv()
        r = rown[own, :] + mrecv[i].astype(f32)
        centre = r - mean(r)
        inv = lax.rsqrt(mean(centre * centre) + eps)
        n2 = centre * inv
        ybuf[i] = (n2 * gm).astype(bf16)
        ycopy(i).start()
        dy = cotv[own, :].astype(f32)
        gbuf[1:2, :] += jnp.sum(dy * n2, axis=0, keepdims=True)
        e = dy * gm
        dr = inv * (e - mean(e) - n2 * mean(e * n2))
        rown[own, :] = dr
        dmb[i, x] = dr.astype(bf16)
        bcopy(i).start()

    def mlp_bwd(i):
        bcopy(i).wait_recv()
        db = dmb[i].reshape(tq, width)
        d = None
        for cc in range(2):
            at = hid_rows(cc, i)
            dh = dot(db, wm[3 * cc + 2], 1, 1)
            dg = (dh * act1[at, :].astype(f32)).astype(bf16)
            du = (dh * act2[at, :].astype(f32)).astype(bf16)
            act1[at, :] = dg
            act2[at, :] = du
            part = dot(dg, wm[3 * cc], 1, 1) + dot(du, wm[3 * cc + 1], 1, 1)
            d = part if d is None else d + part
        tmp[...] = d.reshape(2, cl, width)
        snd2[i] = tmp[ox].astype(bf16)
        own = own_of(i)
        rown[own, :] = rown[own, :] + tmp[x]

    def norm_one(i):
        own = own_of(i)
        dcopy(i).wait_recv()
        dx = rown[own, :] + drecv[i].astype(f32)
        n1 = n1own[own, :]
        gbuf[0:1, :] += jnp.sum(dx * n1, axis=0, keepdims=True)
        e = dx * ga
        dr = inv1own[own, 0:1] * (e - mean(e) - n1 * mean(e * n1))
        rown[own, :] = dr
        dab[i, x] = dr.astype(bf16)
        acopy(i).start()

    kb = min(1024, nkey)

    def attend_back(j, i):
        rows = rows_of(i)

        @when(j == 0)
        def _():
            acopy(i).wait_recv()

        @when(i == 0)
        def _():
            dkv[j % 2] = jnp.zeros(dkv.shape[1:], f32)

        da = dab[i].reshape(tq, width)
        cs = cos_t[:, rows]
        sn = sin_t[:, rows]
        lanes = pl.ds(pl.multiple_of(j * 2 * HEAD, 2 * HEAD), 2 * HEAD)
        dop = dot(da, wo[x, j].reshape(2 * HEAD, width), 1, 1).astype(bf16)
        dof = dop.astype(f32)
        prod = dof * oall[x, rows, lanes].astype(f32)
        dot_t = dof.T.astype(bf16)
        dqs = []
        for par in range(2):
            base = HEAD * (1 - par)
            mine = low_half if par == 0 else jnp.logical_not(low_half)
            neg = -jnp.sum(jnp.where(mine, prod, 0.0), axis=1, keepdims=True)
            hi = neg.astype(bf16).astype(f32)
            lo = neg - hi
            aug = jnp.where(lane == base, hi, jnp.where(lane == base + 1, lo, 0.0))
            doa = jnp.where(mine, dof, aug).astype(bf16)
            qq = qn[par, j, rows, :]
            dq = None
            for b in range(nkey // kb):
                kk = slice(b * kb, (b + 1) * kb)
                p = jnp.exp(dot(qq, kt[j, par, :, kk]))
                d = dot(doa, vt[j, par, :, kk])
                ds = (p * d).astype(bf16)
                pb = p.astype(bf16)
                dkv[j % 2, par, HEAD:, kk] += dot(dot_t[par * HEAD : (par + 1) * HEAD], pb)
                dkv[j % 2, par, :HEAD, kk] += dot(qt[par, j, :, rows], ds)
                part = dot(ds, kt[j, par, :, kk], 1, 1)
                dq = part if dq is None else dq + part
            dqs.append(dq)
        dqt = jnp.where(low_half, dqs[0], dqs[1]).T * 0.125
        at = pl.ds(pl.multiple_of(j * 3 * HEAD, HEAD), HEAD)
        for par in range(2):
            u = rotate(dqt[par * HEAD : (par + 1) * HEAD], cs, sn, -1.0)
            dpt[par, at, rows] = u.astype(bf16)

    g_own = (0, 1, 6)
    g_got = (3, 4, 7)
    g_sent = (2, 5, 8)

    def gcopy(n):
        return remote(wm.at[g_sent[n]], wm.at[g_got[n]], gss.at[n], grs.at[n], core)

    def give(n, dev):
        pl.semaphore_signal(credit.at[n], inc=1, device_id=dev, device_id_type=MESH)

    def tall(ref, cc):
        return ref.at[pl.ds(pl.multiple_of(cc * ntok, ntok), ntok)]

    def grad_into(dst, left, right):
        tile = min(256, width)

        def one(n, carry):
            at = pl.ds(pl.multiple_of(n * tile, tile), tile)
            dst[at, :] = dot(left[:, at], right[...].reshape(ntok, width), 0, 0).astype(bf16)
            return carry

        lax.fori_loop(0, width // tile, one, 0)

    def grad(n):
        left = (x1b, x1b, hid)[n]
        right = (act1, act2, dmb)[n]
        if n < 2:
            grad_into(wm.at[g_sent[n]], left, tall(right, oc))
            grad_into(wm.at[g_own[n]], left, tall(right, c))
            if n == 0:
                pl.semaphore_wait(credit.at[0], 1)
            gcopy(n).start()
        else:
            grad_into(wm.at[g_sent[n]], tall(left, oc), right)
            gcopy(n).start()
            grad_into(wm.at[g_own[n]], tall(left, c), right)
        if n == 2 and ring:
            give(2, zdev)

            @when(outer)
            def _():
                give(2, ydev)

            @when(inner)
            def _():
                give(2, mid)

        if n == 1:
            give(1, core)

            def sent(i, carry):
                bcopy(i).wait_send()
                return carry

            lax.fori_loop(0, NCH, sent, 0)
            if ring:
                give(3, ydev)
                give(3, zdev)

                @when(inner)
                def _():
                    give(3, mid)

    def gsum(n):
        gcopy(n).wait()
        own, got = g_own[n], g_got[n]
        wm[own] = (wm[own].astype(f32) + wm[got].astype(f32)).astype(bf16)
        if n == 2 and ring:
            pl.semaphore_wait(credit.at[2], 2)

    def weights_free():
        give(0, core)

    def buffers_free():
        pl.semaphore_wait(credit.at[1], 1)
        if ring:
            pl.semaphore_wait(credit.at[3], 2 + jnp.where(inner, 1, 0))

    place = jnp.where(y == 0, z, 7 - z)
    seg = fq // 16
    hops = 14

    def ring_row(p):
        p = (p + 8) % 8
        return {"rows": jnp.where(p < 4, 2 * p, 15 - 2 * p)}

    def ring_copies(u, k, to_slot):
        cps = []
        for d in range(2):
            sign = 1 - 2 * d
            at = d * 8 * seg + ((place - sign * k + 16) % 8) * seg
            rows = pl.ds(pl.multiple_of(at, 16), seg)
            if to_slot:
                slot = ((u * 2 + d) * 7 + k) * seg
                part = wm.at[ring_own(u), rows]
                dst = hid.at[pl.ds(pl.multiple_of(slot, 16), seg)]
            else:
                part = dst = wm.at[ring_final(u), rows]
            cps.append(
                remote(part, dst, rss.at[u, d, k], rrs.at[u, d, k], ring_row(place + sign))
            )
        return cps

    def ring_own(u):
        return jnp.where(u == 0, 6, u - 1)

    def ring_final(u):
        return jnp.where(u == 0, 7, u + 2)

    def ring_step(m):
        u = m % 3
        k = m // 3 - RING_LAG * u
        live = jnp.logical_and(k >= 0, k <= hops)

        @when(jnp.logical_and(live, k >= 1))
        def _():
            for cp in ring_copies(u, k - 1, False):
                cp.wait_recv()

        @when(jnp.logical_and(k >= 1, k <= 7))
        def _():
            for d in range(2):
                sign = 1 - 2 * d
                at = d * 8 * seg + ((place - sign * k + 16) % 8) * seg
                rows = pl.ds(pl.multiple_of(at, 16), seg)
                slot = pl.ds(pl.multiple_of(((u * 2 + d) * 7 + k - 1) * seg, 16), seg)
                src = ring_own(u)
                wm[jnp.where(k == 7, ring_final(u), src), rows, :] = (
                    wm[src, rows, :].astype(f32) + hid[slot, :].astype(f32)
                ).astype(bf16)

        @when(jnp.logical_and(live, k <= 6))
        def _():
            for cp in ring_copies(u, k, True):
                cp.start()

        @when(jnp.logical_and(k >= 7, k < hops))
        def _():
            for cp in ring_copies(u, k, False):
                cp.start()

        @when(jnp.logical_and(live, k >= 2))
        def _():
            for cp in ring_copies(u, k - 2, False):
                cp.wait_send()

    sub = 3 * HEAD

    def acore(b):
        src = act2.at[pl.ds(pl.multiple_of((4 + b) * sub, sub), sub)]
        dst = act2.at[pl.ds(pl.multiple_of(b * sub, sub), sub)]
        return remote(src, dst, gss.at[3 + b], grs.at[3 + b], core)

    def asum(b):
        acore(b).wait()
        got = act2[pl.ds(pl.multiple_of(b * sub, sub), sub), :]
        rows = pl.ds(pl.multiple_of(b * sub, sub), sub)
        agrad[rows, :] = (agrad[rows, :].astype(f32) + got.astype(f32)).astype(bf16)

    def astart(b, theirs, ours):
        act2[pl.ds(pl.multiple_of((4 + b) * sub, sub), sub), :] = theirs.astype(bf16)
        acore(b).start()
        agrad[pl.ds(pl.multiple_of(b * sub, sub), sub), :] = ours.astype(bf16)

    hs = sub // 2

    def tree(b, phase):
        mine = agrad.at[pl.ds(pl.multiple_of(b * sub + y * hs, hs), hs)]
        final = act2.at[pl.ds(pl.multiple_of(b * sub + y * hs, hs), hs)]
        buf_a = x1b.at[pl.ds(pl.multiple_of(b * sub, hs), hs)]
        buf_b = x1b.at[pl.ds(pl.multiple_of(b * sub + hs, hs), hs)]
        buf_c = dmb.at[b, 0, pl.ds(0, hs)]
        c0 = lambda: remote(agrad.at[pl.ds(pl.multiple_of(b * sub + (1 - y) * hs, hs), hs)], buf_a, fas.at[b, 0], far.at[b, 0], ydev)
        c1 = lambda: remote(mine, buf_b, fas.at[b, 1], far.at[b, 1], zdev)
        c2 = lambda: remote(mine, buf_c, fas.at[b, 2], far.at[b, 2], mid)
        c3 = lambda: remote(final, final, fas.at[b, 3], far.at[b, 3], zdev)
        c4 = lambda: remote(final, final, fas.at[b, 4], far.at[b, 4], ydev)

        def add(buf, dst):
            dst[...] = (mine[...].astype(f32) + buf[...].astype(f32)).astype(bf16)

        if phase == 0:
            c0().start()
        elif phase == 1:
            c0().wait_recv()
            add(buf_a, mine)

            @when(outer)
            def _():
                c1().start()
        elif phase == 2:

            @when(inner)
            def _():
                c1().wait_recv()
                add(buf_b, mine)
                c2().start()
        elif phase == 3:

            @when(inner)
            def _():
                c2().wait()
                add(buf_c, final)
                c3().start()
                c4().start()
        elif phase == 4:

            @when(outer)
            def _():
                c3().wait_recv()
                c4().start()
        else:
            c4().wait_recv()
            c0().wait_send()
            c4().wait_send()

            @when(outer)
            def _():
                c1().wait_send()

            @when(inner)
            def _():
                c3().wait_send()

    def gain_copy(n):
        return remote(gbuf, grecv.at[n], ns.at[n], nr.at[n], doubling[n])

    def gain_step(n):
        if n > 0:
            gain_copy(n - 1).wait()
            gbuf[...] += grecv[n - 1]
        if n < len(doubling):
            gain_copy(n).start()

    theirs_cols = pl.ds(pl.multiple_of(oc * ntok, ntok), ntok)
    mine_cols = pl.ds(pl.multiple_of(c * ntok, ntok), ntok)

    def kv_rows(j):
        return pl.ds(pl.multiple_of(j * 3 * HEAD + HEAD, HEAD), 2 * HEAD)

    def kvback(j):
        return remote(dpt.at[:, kv_rows(j)], dkvr.at[j], css.at[j], crs.at[j], core)

    def kv_send(j):
        dpt[:, kv_rows(j), :] = dkv[j % 2, :, :, theirs_cols].astype(bf16)
        kvback(j).start()

    def kv_finish(j):
        kvback(j).wait()
        base = j * 3 * HEAD
        for par in range(2):
            u = dkv[j % 2, par, :, mine_cols] + dkvr[j, par].astype(f32)
            dk = rotate(u[:HEAD], cos_t[...], sin_t[...], -1.0)
            dpt[par, pl.ds(pl.multiple_of(base + HEAD, HEAD), HEAD), :] = dk.astype(bf16)
            dpt[par, pl.ds(pl.multiple_of(base + 2 * HEAD, HEAD), HEAD), :] = u[HEAD:].astype(bf16)

    def qkv_grads(j):
        rows = pl.ds(pl.multiple_of(j * sub, HEAD), sub)
        xr = xall[...].reshape(ntok, width)
        astart(1 + j, dot(dpt[oc, rows, :], xr), dot(dpt[c, rows, :], xr))

    def out_grads():
        both = dot(oall[x], dab[...].reshape(ntok, width), 0, 0).reshape(hc, 2, HEAD, width)
        first = both[:, 0].reshape(sub, width)
        second = both[:, 1].reshape(sub, width)
        astart(0, jnp.where(c == 0, second, first), jnp.where(c == 0, first, second))

    def fcopy(i):
        return remote(snd1.at[i], mrecv.at[i], fss.at[i], frs.at[i], xp)

    def input_terms(i, who):
        cols = pl.ds(pl.multiple_of(i * tq + who * cl, cl), cl)
        d = None
        for cc in range(2):
            part = dot(dpt[cc, :, cols], wqt[cc].reshape(3 * qw, width), 0, 0)
            d = part if d is None else d + part
        return d

    def input_send(i):
        mcopy(i).wait_send()
        snd1[i] = input_terms(i, ox).astype(bf16)
        fcopy(i).start()

    def dxcopy(i):
        return pltpu.make_async_copy(ybuf.at[i], out_dx.at[own_of(i)], lsem.at[i])

    def input_finish(i):
        d = input_terms(i, x)
        fcopy(i).wait_recv()
        d = rown[own_of(i), :] + (d + mrecv[i].astype(f32))
        ycopy(i).wait()
        ybuf[i] = d.astype(bf16)
        dxcopy(i).start()

    def kv_done(j):
        kv_finish(j)
        qkv_grads(j)

    handlers = {
        "S0": attend,
        "S1": mlp_fwd,
        "S2": norm_two,
        "S3": mlp_bwd,
        "D": lambda i: dcopy(i).start(),
        "S4": norm_one,
        "S5": lambda q: attend_back(q // NCH, q % NCH),
        "kvs": kv_send,
        "kvf": kv_done,
        "og": lambda i: out_grads(),
        "as": asum,
        "C0": lambda i: weights_free(),
        "C1": lambda i: buffers_free(),
        "I": input_send,
        "F": input_finish,
    }
    for n in range(3):
        handlers["G%d" % n] = functools.partial(lambda n, i: grad(n), n)
        handlers["gs%d" % n] = functools.partial(lambda n, i: gsum(n), n)
    for n in range(len(doubling) + 1):
        handlers["N%d" % n] = functools.partial(lambda n, i: gain_step(n), n)
    if ring:
        for ph in range(6):
            handlers["T%d" % ph] = functools.partial(lambda ph, b: tree(b, ph), ph)

    plan = [(kind, arg) for kind, arg in make_plan(len(doubling)) if kind in handlers or kind == "R"]
    big = []
    count = 0
    for kind, arg in plan:
        if kind == "R":
            count += arg
            big[-1][2] = count
        else:
            big.append([kind, arg, count])

    total_ring = 3 * (hops + 1 + 2 * RING_LAG)
    big[-1][2] = total_ring
    kinds = sorted({b[0] for b in big}, key=[b[0] for b in big].index)

    packed = [
        kinds.index(kind) + 64 * (arg + 16 * min(ends, total_ring)) for kind, arg, ends in big
    ]

    def entry(t):
        value = packed[0]
        for n in range(1, len(packed)):
            value = jnp.where(t >= n, packed[n], value)
        return value % 64, (value // 64) % 16, value // 1024

    def dispatch(code, arg, first, last):
        if last - first == 1:
            handlers[kinds[first]](arg)
            return
        middle = (first + last) // 2

        @when(code < middle)
        def _():
            dispatch(code, arg, first, middle)

        @when(code >= middle)
        def _():
            dispatch(code, arg, middle, last)

    def one_step(t, done):
        code, arg, ends = entry(t)
        dispatch(code, arg, 0, len(kinds))
        if not ring:
            return done

        def ring_one(m, carry):
            ring_step(m)
            return carry

        lax.fori_loop(done, ends, ring_one, 0)
        return ends

    lax.fori_loop(0, len(big), one_step, 0)

    def result_copies():
        first, third = (3, 7) if ring else (0, 6)
        att = act2 if ring else agrad
        cps = [
            pltpu.make_async_copy(wm.at[pl.ds(first, 2)], g_mlp.at[pl.ds(0, 2)], gls.at[0]),
            pltpu.make_async_copy(wm.at[third], g_mlp.at[2], gls.at[1]),
            pltpu.make_async_copy(att.at[pl.ds(0, sub)], g_out, gls.at[2]),
        ]
        for j in range(hc):
            for n in range(3):
                rows = pl.ds((1 + j) * sub + n * HEAD, HEAD)
                cps.append(
                    pltpu.make_async_copy(att.at[rows], g_qkv.at[n, j], gls.at[len(cps)])
                )
        return cps

    for cp in result_copies():
        cp.start()
    g_ga[...] = gbuf[0:1, :]
    g_gm[...] = gbuf[1:2, :]

    for i in range(NCH):
        dxcopy(i).wait()
        xcopy(i).wait_send()
        for cp in kvcopies(i):
            cp.wait_send()
        ocopy(i).wait_send()
        dcopy(i).wait_send()
        acopy(i).wait_send()
        fcopy(i).wait_send()
    for w in (*w_q, w_o, w_ox, w_oxc, w_g, w_u, w_d):
        w.wait_send()
    if ring:
        for u in range(3):
            for cp in ring_copies(u, hops - 1, False):
                cp.wait_send()
    for cp in result_copies():
        cp.wait()


RING_LAG = 1


def make_plan(doublings):
    plan = [
        ("S0", 0), ("S0", 1), ("S0", 2), ("S0", 3), ("S1", 0), ("S1", 1), ("S1", 2), ("S2", 0),
        ("S1", 3), ("S2", 1), ("S2", 2), ("S3", 0), ("S2", 3), ("D", 0), ("S3", 1), ("D", 1),
        ("S3", 2), ("D", 2), ("S3", 3), ("C0", 0), ("D", 3), ("G2", 0), ("S4", 0), ("G0", 0),
        ("gs2", 0), ("R", 3), ("S4", 1), ("S4", 2), ("gs0", 0), ("R", 3), ("S4", 3), ("G1", 0),
        ("R", 2), ("S5", 0), ("N0", 0), ("gs1", 0), ("R", 3), ("C1", 0), ("S5", 1), ("N1", 0),
        ("R", 2), ("S5", 2), ("N2", 0), ("R", 3), ("S5", 3), ("N3", 0), ("R", 2), ("og", 0),
        ("R", 1), ("kvs", 0), ("S5", 4), ("N4", 0), ("R", 3), ("kvf", 0), ("as", 0), ("T0", 0),
        ("S5", 5), ("N5", 0), ("R", 3), ("as", 1), ("T0", 1), ("S5", 6), ("T1", 0), ("S5", 7),
        ("R", 3), ("kvs", 1), ("T2", 0), ("S5", 8), ("T1", 1), ("R", 1), ("kvf", 1), ("R", 1),
        ("S5", 9), ("T2", 1), ("T3", 0), ("R", 2), ("as", 2), ("T0", 2), ("S5", 10), ("R", 1),
        ("S5", 11), ("T1", 2), ("T3", 1), ("T4", 0), ("R", 2), ("kvs", 2), ("R", 1), ("kvf", 2),
        ("T2", 2), ("T5", 0), ("T4", 1), ("I", 0), ("I", 1), ("I", 2), ("R", 1), ("as", 3),
        ("T0", 3), ("I", 3), ("R", 2), ("T3", 2), ("F", 0), ("T5", 1), ("R", 1), ("T1", 3),
        ("T4", 2), ("R", 3), ("F", 1), ("F", 2), ("T5", 2), ("T2", 3), ("R", 2), ("T3", 3),
        ("R", 1), ("F", 3), ("T4", 3), ("R", 4), ("T5", 3), ("R", 1),
    ]
    return plan + [("N%d" % n, 0) for n in range(6, doublings + 1)]


def results_kernel(y, dx, mlp, out, qkv, ga, gm, y2, dx2, gate2, up2, down2, out2, qkv2, ga2, gm2,
                   low, wide, held, in_sem, out_sem, row_sem):
    width, qw = mlp.shape[1], out.shape[0]
    half = width // 2
    pairs = []
    for n, dst in enumerate((gate2, up2, down2)):
        for p in range(2):
            rows = pl.ds(p * half, half)
            pairs.append((mlp.at[n, rows], dst.at[rows], half))
    for n in range(3):
        pairs.append((qkv.at[n], qkv2.at[n], qw))
    pairs.append((out, out2, qw))
    moves = []
    at = 0
    for k, (src, dst, size) in enumerate(pairs):
        part = pl.ds(at, size)
        moves.append((
            pltpu.make_async_copy(src, low.at[part], in_sem.at[k]),
            pltpu.make_async_copy(wide.at[part], dst, out_sem.at[k]),
            slice(at, at + size),
        ))
        at += size
    rows = [
        (
            pltpu.make_async_copy(src, held.at[n], row_sem.at[n]),
            pltpu.make_async_copy(held.at[n], dst, row_sem.at[2 + n]),
        )
        for n, (src, dst) in enumerate(((y, y2), (dx, dx2)))
    ]
    for load, _, _ in moves:
        load.start()
    for load, _ in rows:
        load.start()
    ga2[...] = ga[0]
    gm2[...] = gm[0]
    for load, store, part in moves:
        load.wait()
        wide[part, :] = low[part, :].astype(f32)
        store.start()
    for load, store in rows:
        load.wait()
        store.start()
    for _, store, _ in moves:
        store.wait()
    for _, store in rows:
        store.wait()


def results(y, dx, g_mlp, g_out, g_qkv, g_ga, g_gm):
    _, width, fq = g_mlp.shape
    qw = g_out.shape[0]
    total = 3 * width + 4 * qw
    vmem = pl.BlockSpec(memory_space=pltpu.VMEM)
    hbm = pl.BlockSpec(memory_space=pl.ANY)
    S = jax.ShapeDtypeStruct
    dma = pltpu.SemaphoreType.DMA
    return pl.pallas_call(
        results_kernel,
        out_shape=[
            S(y.shape, bf16), S(dx.shape, bf16), S((width, fq), f32), S((width, fq), f32),
            S((fq, width), f32), S((qw, width), f32), S((3, qw, width), f32),
            S((width,), f32), S((width,), f32),
        ],
        in_specs=[hbm] * 5 + [vmem] * 2,
        out_specs=[hbm] * 7 + [vmem] * 2,
        scratch_shapes=[
            pltpu.VMEM((total, width), bf16), pltpu.VMEM((total, width), f32),
            pltpu.VMEM((2, *y.shape), bf16), dma((10,)), dma((10,)), dma((4,)),
        ],
        compiler_params=pltpu.CompilerParams(vmem_limit_bytes=VLIM),
    )(y, dx, g_mlp, g_out, g_qkv, g_ga, g_gm)


def on_device(
    nrows, tokens, lengths, w_qkv, w_out, w_gate, w_up, w_down, gain_attn, gain_mlp, cotangent
):
    _, length, width = tokens.shape
    qw = w_qkv.shape[2]
    fq = w_gate.shape[1]
    hc = qw // HEAD
    nh = 2 * hc
    cl = length // NCH
    tq = 2 * cl
    ntok = 2 * length
    nkey = 2 * ntok
    cores, chunk, xs, place = np.meshgrid(
        np.arange(2), np.arange(NCH), np.arange(2), np.arange(cl), indexing="ij"
    )
    position = ((2 * xs + cores) * length + chunk * cl + place).reshape(2, ntok)
    half = HEAD // 2
    freqs = rope_base ** (-np.arange(half) / half)
    angles = freqs[None, :, None] * position[:, None, :]
    turns = np.stack([np.cos(angles), np.sin(angles)], axis=1).astype(np.float32)
    places = position.reshape(1, nkey).astype(np.int32)

    hbm = pl.BlockSpec(memory_space=pl.ANY)
    vmem = pl.BlockSpec(memory_space=pltpu.VMEM)
    S = jax.ShapeDtypeStruct
    V = pltpu.VMEM
    dma = pltpu.SemaphoreType.DMA
    doublings = 2 + (nrows - 1).bit_length()
    scratch = [
        V((NCH, 2, cl, width), bf16),
        V((length, width), bf16),
        V((2, hc, 3, HEAD, width), bf16),
        V((2, hc, 2, HEAD, width), bf16),
        V((9, width, fq), bf16),
        V((hc, 2, 2 * HEAD, nkey), bf16),
        V((hc, 2, 2 * HEAD, nkey), bf16),
        V((2, hc, ntok, 2 * HEAD), bf16),
        V((2, hc, HEAD, ntok), bf16),
        V((2, ntok, 2 * qw), bf16),
        V((ntok, width), bf16),
        V((length, width), f32),
        V((length, width), f32),
        V((length, 128), f32),
        V((2 * ntok, fq), bf16),
        V((2 * ntok, fq), bf16),
        V((2 * ntok, fq), bf16),
        V((NCH, 2, cl, width), bf16),
        V((NCH, 2, cl, width), bf16),
        V((NCH, cl, width), bf16),
        V((NCH, cl, width), bf16),
        V((NCH, cl, width), bf16),
        V((NCH, cl, width), bf16),
        V((2, cl, width), f32),
        V((2, cl, 128), f32),
        V((2, 2, 2 * HEAD, nkey), f32),
        V((hc, 2, 2 * HEAD, ntok), bf16),
        V((2, 3 * qw, ntok), bf16),
        V((NCH, cl, width), bf16),
        V(((1 + hc) * 3 * HEAD, width), bf16),
        V((8, width), f32),
        V((doublings, 8, width), f32),
        V((2, HEAD // 2, ntok), f32),
        dma((NCH + 9,)),
        dma((3,)), dma((3,)),
        dma((7,)), dma((7,)),
        dma((NCH,)), dma((NCH,)),
        dma((NCH, 4)), dma((NCH, 4)),
        dma((NCH,)), dma((NCH,)),
        dma((NCH,)), dma((NCH,)),
        dma((NCH,)), dma((NCH,)),
        dma((NCH,)), dma((NCH,)),
        dma((NCH,)), dma((NCH,)),
        dma((hc,)), dma((hc,)),
        dma((NCH,)), dma((NCH,)),
        dma((4 + hc,)), dma((4 + hc,)), dma((3 + 3 * hc,)),
        dma((3, 2, 14)), dma((3, 2, 14)),
        dma((1 + hc, 5)), dma((1 + hc, 5)),
        dma((doublings,)), dma((doublings,)),
        dma((NCH,)),
        pltpu.SemaphoreType.REGULAR((4,)),
    ]
    outs = pl.pallas_call(
        functools.partial(layer_kernel, nrows),
        out_shape=[
            S((length, width), bf16), S((length, width), bf16),
            S((3, width, fq), bf16), S((qw, width), bf16), S((3, hc, HEAD, width), bf16),
            S((1, width), f32), S((1, width), f32),
        ],
        in_specs=[hbm] * 8 + [pl.BlockSpec(memory_space=pltpu.SMEM)] + [vmem] * 3,
        out_specs=[hbm] * 5 + [vmem] * 2,
        scratch_shapes=scratch,
        compiler_params=pltpu.CompilerParams(
            collective_id=0, has_side_effects=True, vmem_limit_bytes=VLIM
        ),
    )(
        tokens[0], cotangent[0],
        w_qkv.transpose(0, 2, 1).reshape(3, hc, HEAD, width), w_out.reshape(hc, HEAD, width), w_gate, w_up, w_down,
        jnp.asarray(turns), lengths, gain_attn, gain_mlp, jnp.asarray(places),
    )
    y, dx, g_mlp, g_out, g_qkv, g_ga, g_gm = outs
    if nrows != 8:
        g_mlp, g_out, g_qkv = lax.psum((g_mlp, g_out, g_qkv), "rows")
    y, dx, gate2, up2, down2, out2, qkv2, g_ga, g_gm = results(
        y, dx, g_mlp, g_out, g_qkv.reshape(3, qw, width), g_ga, g_gm
    )
    return (
        y[None], dx[None], qkv2.transpose(0, 2, 1), out2, gate2, up2, down2, g_ga, g_gm,
    )


VLIM = 64 * 2**20


def solution(mesh):
    in_specs = (
        P("rows", "heads", None),
        P("rows"),
        P(None, None, "heads"),
        P("heads", None),
        P(None, "heads"),
        P(None, "heads"),
        P("heads", None),
        P(),
        P(),
        P("rows", "heads", None),
    )
    out_specs = (
        P("rows", "heads", None),
        P("rows", "heads", None),
        P(None, None, "heads"),
        P("heads", None),
        P(None, "heads"),
        P(None, "heads"),
        P("heads", None),
        P(),
        P(),
    )
    return jax.shard_map(
        functools.partial(on_device, mesh.shape["rows"]), mesh=mesh, in_specs=in_specs, out_specs=out_specs, check_vma=False
    )
```

```python
import functools

import jax
import jax.numpy as jnp
import numpy as np
from jax import lax
from jax.experimental import pallas as pl
from jax.experimental.pallas import tpu as pltpu
from jax.sharding import PartitionSpec as P

HEAD = 64
eps = 1e-05
rope_base = 1000.0
MESH = pl.DeviceIdType.MESH
f32 = jnp.float32
bf16 = jnp.bfloat16
NCH = 4


def dot(a, b, ca=1, cb=0):
    return lax.dot_general(a, b, (((ca,), (cb,)), ((), ())), preferred_element_type=f32)


def mean(a):
    return jnp.mean(a, axis=-1, keepdims=True)


def layer_kernel(
    nrows, tok, cot, wq_in, wo_in, wg_in, wu_in, wd_in, turns, lengths, ga_in, gm_in, place_in,
    out_y, out_dx, g_mlp, g_out, g_qkv, g_ga, g_gm,
    xall, cotv, wqt, wo, wm, kt, vt, qn, qt, oall, x1b, rown, n1own, inv1own,
    act1, act2, hid, dmb, dab, mrecv, drecv, snd1, snd2, tmp, itmp,
    dkv, dkvr, dpt, ybuf, agrad, gbuf, grecv, turn,
    lsem, wqs, wqr, wss, wrs, xss, xrs, kss, krs, oss, ors, mss, mrs, bss, brs, dss, drs, ass_, ars,
    css, crs, fss, frs, gss, grs, gls, rss, rrs, fas, far, ns, nr, ysem, credit,
):
    ring = nrows == 8
    length, width = tok.shape
    cl = length // NCH
    tq = 2 * cl
    ntok = 2 * length
    nkey = 2 * ntok
    hc = wo_in.shape[0]
    qw = hc * HEAD
    fq = wg_in.shape[1]

    h = lax.axis_index("heads")
    r = lax.axis_index("rows")
    x = h // 2
    c = h % 2
    oc = 1 - c
    ox = 1 - x
    core = {"heads": h + 1 - 2 * c}
    xp = {"heads": h + 2 - 4 * x}
    y = r % 2
    z = r // 2
    outer = jnp.logical_or(z == 0, z == 3)
    inner = jnp.logical_not(outer)
    ydev = {"rows": r + 1 - 2 * y}
    zdev = {"rows": r + 2 - 4 * (z % 2)}
    mid = {"rows": (3 - z) * 2 + y}
    doubling = [core, xp]
    span = 1
    while span < nrows:
        doubling.append({"rows": r + span - 2 * span * ((r // span) % 2)})
        span *= 2

    def when(cond):
        return pl.when(cond)

    def remote(src, dst, ss, rs, dev):
        return pltpu.make_async_remote_copy(
            src_ref=src, dst_ref=dst, send_sem=ss, recv_sem=rs, device_id=dev, device_id_type=MESH
        )

    barrier = pltpu.get_barrier_semaphore()
    for dev in doubling:
        pl.semaphore_signal(barrier, inc=1, device_id=dev, device_id_type=MESH)
    greeted = len(doubling)
    if ring:

        @when(inner)
        def _():
            pl.semaphore_signal(barrier, inc=1, device_id=mid, device_id_type=MESH)

        greeted = greeted + jnp.where(inner, 1, 0)

    def local_copies():
        cps = []
        for i in range(NCH):
            cps.append(pltpu.make_async_copy(tok.at[pl.ds(i * cl, cl)], xall.at[i, x], lsem.at[i]))
        n = NCH
        for src, dst in (
            (wq_in.at[0], wqt.at[c, :, 0]), (wq_in.at[1], wqt.at[c, :, 1]),
            (wq_in.at[2], wqt.at[c, :, 2]), (turns.at[c], turn), (wo_in, wo.at[x, :, c]), (wg_in, wm.at[3 * c]),
            (wu_in, wm.at[3 * c + 1]), (wd_in, wm.at[3 * c + 2]), (cot, cotv),
        ):
            cps.append(pltpu.make_async_copy(src, dst, lsem.at[n]))
            n += 1
        return cps

    locals_ = local_copies()
    for cp in locals_:
        cp.start()

    pl.semaphore_wait(barrier, greeted)

    def xcopy(i):
        return remote(tok.at[pl.ds(i * cl, cl)], xall.at[i, x], xss.at[i], xrs.at[i], xp)

    w_q = [
        remote(wq_in.at[n], wqt.at[c, :, n], wqs.at[n], wqr.at[n], core) for n in range(3)
    ]
    w_o = remote(wo_in, wo.at[x, :, c], wss.at[1], wrs.at[1], core)
    w_ox = remote(wo_in, wo.at[x, :, c], wss.at[2], wrs.at[2], xp)
    w_oxc = remote(wo.at[ox, :, c], wo.at[ox, :, c], wss.at[3], wrs.at[3], core)
    w_g = remote(wg_in, wm.at[3 * c], wss.at[4], wrs.at[4], core)
    w_u = remote(wu_in, wm.at[3 * c + 1], wss.at[5], wrs.at[5], core)
    w_d = remote(wd_in, wm.at[3 * c + 2], wss.at[6], wrs.at[6], core)
    for w in w_q:
        w.start()
    for i in range(NCH):
        xcopy(i).start()
    w_o.start()
    w_g.start()
    w_u.start()
    w_d.start()
    w_ox.start()

    nrow = lax.broadcasted_iota(jnp.int32, (HEAD, nkey), 0)
    vrows = jnp.where(nrow < 2, 1.0, 0.0).astype(bf16)
    valid = place_in[...] < lengths[0]
    augk = jnp.where(
        nrow == 0, jnp.where(valid, 0.0, -1e30), jnp.where(nrow < 4, 1.0, 0.0)
    ).astype(bf16)
    ga = ga_in[...].reshape(1, width)
    gm = gm_in[...].reshape(1, width)
    cos_t, sin_t = turn.at[0], turn.at[1]
    for pr in range(hc):
        kt[pr, 0, HEAD:, :] = augk
        kt[pr, 1, :HEAD, :] = augk
        vt[pr, 0, HEAD:, :] = vrows
        vt[pr, 1, :HEAD, :] = vrows
    gbuf[...] = jnp.zeros_like(gbuf)

    lane = lax.broadcasted_iota(jnp.int32, (tq, 2 * HEAD), 1)
    low_half = lane < HEAD

    def rotate(u, cs, sn, sign):
        half = HEAD // 2
        a, b = u[:half], u[half:]
        return jnp.concatenate([a * cs - sign * (b * sn), b * cs + sign * (a * sn)], axis=0)

    def kvcopies(i):
        cps = []
        cols = pl.ds(pl.multiple_of(c * ntok + i * tq, tq), tq)
        n = 0
        for ref in (kt, vt):
            for par in range(2):
                part = ref.at[:, par, pl.ds(par * HEAD, HEAD), cols]
                cps.append(remote(part, part, kss.at[i, n], krs.at[i, n], core))
                n += 1
        return cps

    for cp in locals_[NCH : NCH + 4]:
        cp.wait()
    for w in w_q:
        w.wait_recv()

    def qkv(i, carry):
        pltpu.make_async_copy(tok.at[pl.ds(i * cl, cl)], xall.at[i, x], lsem.at[i]).wait()
        xcopy(i).wait_recv()
        xb = xall[i].reshape(tq, width)
        here = pl.ds(pl.multiple_of(i * tq, tq), tq)
        cols = pl.ds(pl.multiple_of(c * ntok + i * tq, tq), tq)
        cs = cos_t[:, here]
        sn = sin_t[:, here]
        for cc in range(2):
            pt = dot(wqt[cc].reshape(3 * qw, width), xb, 1, 1)
            at = slice(cc * HEAD, cc * HEAD + HEAD)
            for j in range(hc):
                u = pt[j * 3 * HEAD : (j + 1) * 3 * HEAD]
                q = rotate(u[:HEAD], cs, sn, 1.0).astype(bf16)
                qt[cc, j, :, here] = (q.astype(f32) * 0.125).astype(bf16)
                kt[j, cc, at, cols] = rotate(u[HEAD : 2 * HEAD], cs, sn, 1.0).astype(bf16)
                vt[j, cc, at, cols] = u[2 * HEAD :].astype(bf16)
        for cp in kvcopies(i):
            cp.start()
        for j in range(hc):
            both = jnp.concatenate([qt[0, j, :, here], qt[1, j, :, here]], axis=0)
            nat = both.astype(f32).T
            qn[0, j, here, :] = jnp.where(
                low_half, nat, jnp.where(lane == HEAD, 1.0, 0.0)
            ).astype(bf16)
            qn[1, j, here, :] = jnp.where(
                low_half, jnp.where(lane == 0, 1.0, 0.0), nat
            ).astype(bf16)
        return carry

    lax.fori_loop(0, NCH, qkv, 0)

    def kvwait(i, carry):
        for cp in kvcopies(i):
            cp.wait_recv()
        return carry

    lax.fori_loop(0, NCH, kvwait, 0)
    w_ox.wait_recv()
    w_oxc.start()
    for cp in locals_[NCH + 4 :]:
        cp.wait()
    for w in (w_o, w_oxc, w_g, w_u, w_d):
        w.wait_recv()

    def rows_of(i):
        return pl.ds(pl.multiple_of(i * tq, tq), tq)

    def hid_rows(cc, i):
        return pl.ds(pl.multiple_of(cc * ntok + i * tq, tq), tq)

    def own_of(i):
        return pl.ds(pl.multiple_of(i * cl, cl), cl)

    def ocopy(i):
        part = oall.at[x, rows_of(i)]
        return remote(part, part, oss.at[i], ors.at[i], xp)

    def mcopy(i):
        return remote(snd1.at[i], mrecv.at[i], mss.at[i], mrs.at[i], xp)

    def bcopy(i):
        return remote(dmb.at[i, x], dmb.at[i, x], bss.at[i], brs.at[i], xp)

    def dcopy(i):
        return remote(snd2.at[i], drecv.at[i], dss.at[i], drs.at[i], xp)

    def acopy(i):
        return remote(dab.at[i, x], dab.at[i, x], ass_.at[i], ars.at[i], xp)

    def ycopy(i):
        return pltpu.make_async_copy(ybuf.at[i], out_y.at[own_of(i)], ysem.at[i])

    def attend(i):
        rows = rows_of(i)
        for j in range(hc):
            outs = []
            for par in range(2):
                base = HEAD * (1 - par)
                qq = qn[par, j, rows, :]
                s = dot(qq, kt[j, par])
                top = jnp.max(s, axis=1, keepdims=True)
                p = jnp.exp(s - top).astype(bf16)
                oo = dot(p, vt[j, par], 1, 1)
                total = oo[:, base : base + 1]
                outs.append(oo * (1.0 / total))
                neg = -(top + jnp.log(total))
                hi = neg.astype(bf16).astype(f32)
                mid = (neg - hi).astype(bf16).astype(f32)
                lo = neg - hi - mid
                qf = qq.astype(f32)
                qf = jnp.where(lane == base + 1, hi, qf)
                qf = jnp.where(lane == base + 2, mid, qf)
                qf = jnp.where(lane == base + 3, lo, qf)
                qn[par, j, rows, :] = qf.astype(bf16)
            oall[x, rows, j * 2 * HEAD : (j + 1) * 2 * HEAD] = jnp.where(
                low_half, outs[0], outs[1]
            ).astype(bf16)
        ocopy(i).start()

    def mlp_fwd(i):
        rows, own = rows_of(i), own_of(i)
        ocopy(i).wait_recv()
        a = dot(oall[0, rows, :], wo[0].reshape(2 * qw, width))
        a += dot(oall[1, rows, :], wo[1].reshape(2 * qw, width))
        r = xall[i].reshape(tq, width).astype(f32) + a
        centre = r - mean(r)
        inv = lax.rsqrt(mean(centre * centre) + eps)
        n1 = centre * inv
        tmp[...] = n1.reshape(2, cl, width)
        n1own[own, :] = tmp[x]
        itmp[...] = jnp.broadcast_to(inv, (tq, 128)).reshape(2, cl, 128)
        inv1own[own, :] = itmp[x]
        x1 = n1 * ga
        xb = x1.astype(bf16)
        x1b[rows, :] = xb
        m = None
        for cc in range(2):
            g = dot(xb, wm[3 * cc])
            u = dot(xb, wm[3 * cc + 1])
            sg = 0.5 * jnp.tanh(0.5 * g) + 0.5
            si = g * sg
            hv = (si * u).astype(bf16)
            at = hid_rows(cc, i)
            act2[at, :] = si.astype(bf16)
            act1[at, :] = (u * (sg + si * (1.0 - sg))).astype(bf16)
            hid[at, :] = hv
            part = dot(hv, wm[3 * cc + 2])
            m = part if m is None else m + part
        tmp[...] = m.reshape(2, cl, width)
        snd1[i] = tmp[ox].astype(bf16)
        mcopy(i).start()
        tmp[...] = (x1 + m).reshape(2, cl, width)
        rown[own, :] = tmp[x]

    def norm_two(i):
        own = own_of(i)
        mcopy(i).wait_recv()
        r = rown[own, :] + mrecv[i].astype(f32)
        centre = r - mean(r)
        inv = lax.rsqrt(mean(centre * centre) + eps)
        n2 = centre * inv
        ybuf[i] = (n2 * gm).astype(bf16)
        ycopy(i).start()
        dy = cotv[own, :].astype(f32)
        gbuf[1:2, :] += jnp.sum(dy * n2, axis=0, keepdims=True)
        e = dy * gm
        dr = inv * (e - mean(e) - n2 * mean(e * n2))
        rown[own, :] = dr
        dmb[i, x] = dr.astype(bf16)
        bcopy(i).start()

    def mlp_bwd(i):
        bcopy(i).wait_recv()
        db = dmb[i].reshape(tq, width)
        d = None
        for cc in range(2):
            at = hid_rows(cc, i)
            dh = dot(db, wm[3 * cc + 2], 1, 1)
            dg = (dh * act1[at, :].astype(f32)).astype(bf16)
            du = (dh * act2[at, :].astype(f32)).astype(bf16)
            act1[at, :] = dg
            act2[at, :] = du
            part = dot(dg, wm[3 * cc], 1, 1) + dot(du, wm[3 * cc + 1], 1, 1)
            d = part if d is None else d + part
        tmp[...] = d.reshape(2, cl, width)
        snd2[i] = tmp[ox].astype(bf16)
        own = own_of(i)
        rown[own, :] = rown[own, :] + tmp[x]

    def norm_one(i):
        own = own_of(i)
        dcopy(i).wait_recv()
        dx = rown[own, :] + drecv[i].astype(f32)
        n1 = n1own[own, :]
        gbuf[0:1, :] += jnp.sum(dx * n1, axis=0, keepdims=True)
        e = dx * ga
        dr = inv1own[own, 0:1] * (e - mean(e) - n1 * mean(e * n1))
        rown[own, :] = dr
        dab[i, x] = dr.astype(bf16)
        acopy(i).start()

    kb = min(2048, nkey)

    def attend_back(j, i):
        rows = rows_of(i)

        @when(j == 0)
        def _():
            acopy(i).wait_recv()

        @when(i == 0)
        def _():
            dkv[j % 2] = jnp.zeros(dkv.shape[1:], f32)

        da = dab[i].reshape(tq, width)
        cs = cos_t[:, rows]
        sn = sin_t[:, rows]
        lanes = pl.ds(pl.multiple_of(j * 2 * HEAD, 2 * HEAD), 2 * HEAD)
        dop = dot(da, wo[x, j].reshape(2 * HEAD, width), 1, 1).astype(bf16)
        dof = dop.astype(f32)
        prod = dof * oall[x, rows, lanes].astype(f32)
        dot_t = dof.T.astype(bf16)
        dqs = []
        for par in range(2):
            base = HEAD * (1 - par)
            mine = low_half if par == 0 else jnp.logical_not(low_half)
            neg = -jnp.sum(jnp.where(mine, prod, 0.0), axis=1, keepdims=True)
            hi = neg.astype(bf16).astype(f32)
            lo = neg - hi
            aug = jnp.where(lane == base, hi, jnp.where(lane == base + 1, lo, 0.0))
            doa = jnp.where(mine, dof, aug).astype(bf16)
            qq = qn[par, j, rows, :]
            dq = None
            for b in range(nkey // kb):
                kk = slice(b * kb, (b + 1) * kb)
                p = jnp.exp(dot(qq, kt[j, par, :, kk]))
                d = dot(doa, vt[j, par, :, kk])
                ds = (p * d).astype(bf16)
                pb = p.astype(bf16)
                dkv[j % 2, par, HEAD:, kk] += dot(dot_t[par * HEAD : (par + 1) * HEAD], pb)
                dkv[j % 2, par, :HEAD, kk] += dot(qt[par, j, :, rows], ds)
                part = dot(ds, kt[j, par, :, kk], 1, 1)
                dq = part if dq is None else dq + part
            dqs.append(dq)
        dqt = jnp.where(low_half, dqs[0], dqs[1]).T * 0.125
        at = pl.ds(pl.multiple_of(j * 3 * HEAD, HEAD), HEAD)
        for par in range(2):
            u = rotate(dqt[par * HEAD : (par + 1) * HEAD], cs, sn, -1.0)
            dpt[par, at, rows] = u.astype(bf16)

    g_own = (0, 1, 6)
    g_got = (3, 4, 7)
    g_sent = (2, 5, 8)

    def gcopy(n):
        return remote(wm.at[g_sent[n]], wm.at[g_got[n]], gss.at[n], grs.at[n], core)

    def give(n, dev):
        pl.semaphore_signal(credit.at[n], inc=1, device_id=dev, device_id_type=MESH)

    def tall(ref, cc):
        return ref.at[pl.ds(pl.multiple_of(cc * ntok, ntok), ntok)]

    def grad_into(dst, left, right):
        tile = min(256, width)

        def one(n, carry):
            at = pl.ds(pl.multiple_of(n * tile, tile), tile)
            dst[at, :] = dot(left[:, at], right[...].reshape(ntok, width), 0, 0).astype(bf16)
            return carry

        lax.fori_loop(0, width // tile, one, 0)

    def grad(n):
        left = (x1b, x1b, hid)[n]
        right = (act1, act2, dmb)[n]
        if n < 2:
            grad_into(wm.at[g_sent[n]], left, tall(right, oc))
            grad_into(wm.at[g_own[n]], left, tall(right, c))
            if n == 0:
                pl.semaphore_wait(credit.at[0], 1)
            gcopy(n).start()
        else:
            grad_into(wm.at[g_sent[n]], tall(left, oc), right)
            gcopy(n).start()
            grad_into(wm.at[g_own[n]], tall(left, c), right)
        if n == 2 and ring:
            give(2, zdev)

            @when(outer)
            def _():
                give(2, ydev)

            @when(inner)
            def _():
                give(2, mid)

        if n == 1:
            give(1, core)

            def sent(i, carry):
                bcopy(i).wait_send()
                return carry

            lax.fori_loop(0, NCH, sent, 0)
            if ring:
                give(3, ydev)
                give(3, zdev)

                @when(inner)
                def _():
                    give(3, mid)

    def gsum(n):
        gcopy(n).wait()
        own, got = g_own[n], g_got[n]
        wm[own] = (wm[own].astype(f32) + wm[got].astype(f32)).astype(bf16)
        if n == 2 and ring:
            pl.semaphore_wait(credit.at[2], 2)

    def weights_free():
        give(0, core)

    def buffers_free():
        pl.semaphore_wait(credit.at[1], 1)
        if ring:
            pl.semaphore_wait(credit.at[3], 2 + jnp.where(inner, 1, 0))

    place = jnp.where(y == 0, z, 7 - z)
    seg = fq // 16
    hops = 14

    def ring_row(p):
        p = (p + 8) % 8
        return {"rows": jnp.where(p < 4, 2 * p, 15 - 2 * p)}

    def ring_copies(u, k, to_slot):
        cps = []
        for d in range(2):
            sign = 1 - 2 * d
            at = d * 8 * seg + ((place - sign * k + 16) % 8) * seg
            rows = pl.ds(pl.multiple_of(at, 16), seg)
            if to_slot:
                slot = ((u * 2 + d) * 7 + k) * seg
                part = wm.at[ring_own(u), rows]
                dst = hid.at[pl.ds(pl.multiple_of(slot, 16), seg)]
            else:
                part = dst = wm.at[ring_final(u), rows]
            cps.append(
                remote(part, dst, rss.at[u, d, k], rrs.at[u, d, k], ring_row(place + sign))
            )
        return cps

    def ring_own(u):
        return jnp.where(u == 0, 6, u - 1)

    def ring_final(u):
        return jnp.where(u == 0, 7, u + 2)

    def ring_step(m):
        u = m % 3
        k = m // 3 - RING_LAG * u
        live = jnp.logical_and(k >= 0, k <= hops)

        @when(jnp.logical_and(live, k >= 1))
        def _():
            for cp in ring_copies(u, k - 1, False):
                cp.wait_recv()

        @when(jnp.logical_and(k >= 1, k <= 7))
        def _():
            for d in range(2):
                sign = 1 - 2 * d
                at = d * 8 * seg + ((place - sign * k + 16) % 8) * seg
                rows = pl.ds(pl.multiple_of(at, 16), seg)
                slot = pl.ds(pl.multiple_of(((u * 2 + d) * 7 + k - 1) * seg, 16), seg)
                src = ring_own(u)
                wm[jnp.where(k == 7, ring_final(u), src), rows, :] = (
                    wm[src, rows, :].astype(f32) + hid[slot, :].astype(f32)
                ).astype(bf16)

        @when(jnp.logical_and(live, k <= 6))
        def _():
            for cp in ring_copies(u, k, True):
                cp.start()

        @when(jnp.logical_and(k >= 7, k < hops))
        def _():
            for cp in ring_copies(u, k, False):
                cp.start()

        @when(jnp.logical_and(live, k >= 2))
        def _():
            for cp in ring_copies(u, k - 2, False):
                cp.wait_send()

    sub = 3 * HEAD

    def acore(b):
        src = act2.at[pl.ds(pl.multiple_of((4 + b) * sub, sub), sub)]
        dst = act2.at[pl.ds(pl.multiple_of(b * sub, sub), sub)]
        return remote(src, dst, gss.at[3 + b], grs.at[3 + b], core)

    def asum(b):
        acore(b).wait()
        got = act2[pl.ds(pl.multiple_of(b * sub, sub), sub), :]
        rows = pl.ds(pl.multiple_of(b * sub, sub), sub)
        agrad[rows, :] = (agrad[rows, :].astype(f32) + got.astype(f32)).astype(bf16)

    def astart(b, theirs, ours):
        act2[pl.ds(pl.multiple_of((4 + b) * sub, sub), sub), :] = theirs.astype(bf16)
        acore(b).start()
        agrad[pl.ds(pl.multiple_of(b * sub, sub), sub), :] = ours.astype(bf16)

    hs = sub // 2

    def tree(b, phase):
        mine = agrad.at[pl.ds(pl.multiple_of(b * sub + y * hs, hs), hs)]
        final = act2.at[pl.ds(pl.multiple_of(b * sub + y * hs, hs), hs)]
        buf_a = x1b.at[pl.ds(pl.multiple_of(b * sub, hs), hs)]
        buf_b = x1b.at[pl.ds(pl.multiple_of(b * sub + hs, hs), hs)]
        buf_c = dmb.at[b, 0, pl.ds(0, hs)]
        c0 = lambda: remote(agrad.at[pl.ds(pl.multiple_of(b * sub + (1 - y) * hs, hs), hs)], buf_a, fas.at[b, 0], far.at[b, 0], ydev)
        c1 = lambda: remote(mine, buf_b, fas.at[b, 1], far.at[b, 1], zdev)
        c2 = lambda: remote(mine, buf_c, fas.at[b, 2], far.at[b, 2], mid)
        c3 = lambda: remote(final, final, fas.at[b, 3], far.at[b, 3], zdev)
        c4 = lambda: remote(final, final, fas.at[b, 4], far.at[b, 4], ydev)

        def add(buf, dst):
            dst[...] = (mine[...].astype(f32) + buf[...].astype(f32)).astype(bf16)

        if phase == 0:
            c0().start()
        elif phase == 1:
            c0().wait_recv()
            add(buf_a, mine)

            @when(outer)
            def _():
                c1().start()
        elif phase == 2:

            @when(inner)
            def _():
                c1().wait_recv()
                add(buf_b, mine)
                c2().start()
        elif phase == 3:

            @when(inner)
            def _():
                c2().wait()
                add(buf_c, final)
                c3().start()
                c4().start()
        elif phase == 4:

            @when(outer)
            def _():
                c3().wait_recv()
                c4().start()
        else:
            c4().wait_recv()
            c0().wait_send()
            c4().wait_send()

            @when(outer)
            def _():
                c1().wait_send()

            @when(inner)
            def _():
                c3().wait_send()

    def gain_copy(n):
        return remote(gbuf, grecv.at[n], ns.at[n], nr.at[n], doubling[n])

    def gain_step(n):
        if n > 0:
            gain_copy(n - 1).wait()
            gbuf[...] += grecv[n - 1]
        if n < len(doubling):
            gain_copy(n).start()

    theirs_cols = pl.ds(pl.multiple_of(oc * ntok, ntok), ntok)
    mine_cols = pl.ds(pl.multiple_of(c * ntok, ntok), ntok)

    def kv_rows(j):
        return pl.ds(pl.multiple_of(j * 3 * HEAD + HEAD, HEAD), 2 * HEAD)

    def kvback(j):
        return remote(dpt.at[:, kv_rows(j)], dkvr.at[j], css.at[j], crs.at[j], core)

    def kv_send(j):
        dpt[:, kv_rows(j), :] = dkv[j % 2, :, :, theirs_cols].astype(bf16)
        kvback(j).start()

    def kv_finish(j):
        kvback(j).wait()
        base = j * 3 * HEAD
        for par in range(2):
            u = dkv[j % 2, par, :, mine_cols] + dkvr[j, par].astype(f32)
            dk = rotate(u[:HEAD], cos_t[...], sin_t[...], -1.0)
            dpt[par, pl.ds(pl.multiple_of(base + HEAD, HEAD), HEAD), :] = dk.astype(bf16)
            dpt[par, pl.ds(pl.multiple_of(base + 2 * HEAD, HEAD), HEAD), :] = u[HEAD:].astype(bf16)

    def qkv_grads(j):
        rows = pl.ds(pl.multiple_of(j * sub, HEAD), sub)
        xr = xall[...].reshape(ntok, width)
        astart(1 + j, dot(dpt[oc, rows, :], xr), dot(dpt[c, rows, :], xr))

    def out_grads():
        both = dot(oall[x], dab[...].reshape(ntok, width), 0, 0).reshape(hc, 2, HEAD, width)
        first = both[:, 0].reshape(sub, width)
        second = both[:, 1].reshape(sub, width)
        astart(0, jnp.where(c == 0, second, first), jnp.where(c == 0, first, second))

    def fcopy(i):
        return remote(snd1.at[i], mrecv.at[i], fss.at[i], frs.at[i], xp)

    def input_terms(i, who):
        cols = pl.ds(pl.multiple_of(i * tq + who * cl, cl), cl)
        d = None
        for cc in range(2):
            part = dot(dpt[cc, :, cols], wqt[cc].reshape(3 * qw, width), 0, 0)
            d = part if d is None else d + part
        return d

    def input_send(i):
        mcopy(i).wait_send()
        snd1[i] = input_terms(i, ox).astype(bf16)
        fcopy(i).start()

    def dxcopy(i):
        return pltpu.make_async_copy(ybuf.at[i], out_dx.at[own_of(i)], lsem.at[i])

    def input_finish(i):
        d = input_terms(i, x)
        fcopy(i).wait_recv()
        d = rown[own_of(i), :] + (d + mrecv[i].astype(f32))
        ycopy(i).wait()
        ybuf[i] = d.astype(bf16)
        dxcopy(i).start()

    def kv_done(j):
        kv_finish(j)
        qkv_grads(j)

    handlers = {
        "S0": attend,
        "S1": mlp_fwd,
        "S2": norm_two,
        "S3": mlp_bwd,
        "D": lambda i: dcopy(i).start(),
        "S4": norm_one,
        "S5": lambda q: attend_back(q // NCH, q % NCH),
        "kvs": kv_send,
        "kvf": kv_done,
        "og": lambda i: out_grads(),
        "as": asum,
        "C0": lambda i: weights_free(),
        "C1": lambda i: buffers_free(),
        "I": input_send,
        "F": input_finish,
    }
    for n in range(3):
        handlers["G%d" % n] = functools.partial(lambda n, i: grad(n), n)
        handlers["gs%d" % n] = functools.partial(lambda n, i: gsum(n), n)
    for n in range(len(doubling) + 1):
        handlers["N%d" % n] = functools.partial(lambda n, i: gain_step(n), n)
    if ring:
        for ph in range(6):
            handlers["T%d" % ph] = functools.partial(lambda ph, b: tree(b, ph), ph)

    plan = [(kind, arg) for kind, arg in make_plan(len(doubling)) if kind in handlers or kind == "R"]
    big = []
    count = 0
    for kind, arg in plan:
        if kind == "R":
            count += arg
            big[-1][2] = count
        else:
            big.append([kind, arg, count])

    total_ring = 3 * (hops + 1 + 2 * RING_LAG)
    big[-1][2] = total_ring
    kinds = sorted({b[0] for b in big}, key=[b[0] for b in big].index)

    packed = [
        kinds.index(kind) + 64 * (arg + 16 * min(ends, total_ring)) for kind, arg, ends in big
    ]

    def entry(t):
        value = packed[0]
        for n in range(1, len(packed)):
            value = jnp.where(t >= n, packed[n], value)
        return value % 64, (value // 64) % 16, value // 1024

    def dispatch(code, arg, first, last):
        if last - first == 1:
            handlers[kinds[first]](arg)
            return
        middle = (first + last) // 2

        @when(code < middle)
        def _():
            dispatch(code, arg, first, middle)

        @when(code >= middle)
        def _():
            dispatch(code, arg, middle, last)

    def one_step(t, done):
        code, arg, ends = entry(t)
        dispatch(code, arg, 0, len(kinds))
        if not ring:
            return done

        def ring_one(m, carry):
            ring_step(m)
            return carry

        lax.fori_loop(done, ends, ring_one, 0)
        return ends

    lax.fori_loop(0, len(big), one_step, 0)

    def result_copies():
        first, third = (3, 7) if ring else (0, 6)
        att = act2 if ring else agrad
        cps = [
            pltpu.make_async_copy(wm.at[pl.ds(first, 2)], g_mlp.at[pl.ds(0, 2)], gls.at[0]),
            pltpu.make_async_copy(wm.at[third], g_mlp.at[2], gls.at[1]),
            pltpu.make_async_copy(att.at[pl.ds(0, sub)], g_out, gls.at[2]),
        ]
        for j in range(hc):
            for n in range(3):
                rows = pl.ds((1 + j) * sub + n * HEAD, HEAD)
                cps.append(
                    pltpu.make_async_copy(att.at[rows], g_qkv.at[n, j], gls.at[len(cps)])
                )
        return cps

    for cp in result_copies():
        cp.start()
    g_ga[...] = gbuf[0:1, :]
    g_gm[...] = gbuf[1:2, :]

    for i in range(NCH):
        dxcopy(i).wait()
        xcopy(i).wait_send()
        for cp in kvcopies(i):
            cp.wait_send()
        ocopy(i).wait_send()
        dcopy(i).wait_send()
        acopy(i).wait_send()
        fcopy(i).wait_send()
    for w in (*w_q, w_o, w_ox, w_oxc, w_g, w_u, w_d):
        w.wait_send()
    if ring:
        for u in range(3):
            for cp in ring_copies(u, hops - 1, False):
                cp.wait_send()
    for cp in result_copies():
        cp.wait()


RING_LAG = 1


def make_plan(doublings):
    plan = [
        ("S0", 0), ("S0", 1), ("S0", 2), ("S0", 3), ("S1", 0), ("S1", 1), ("S1", 2), ("S2", 0),
        ("S1", 3), ("S2", 1), ("S2", 2), ("S3", 0), ("S2", 3), ("D", 0), ("S3", 1), ("D", 1),
        ("S3", 2), ("D", 2), ("S3", 3), ("C0", 0), ("D", 3), ("G2", 0), ("S4", 0), ("G0", 0),
        ("gs2", 0), ("R", 3), ("S4", 1), ("S4", 2), ("gs0", 0), ("R", 3), ("S4", 3), ("G1", 0),
        ("R", 2), ("S5", 0), ("N0", 0), ("gs1", 0), ("R", 3), ("C1", 0), ("S5", 1), ("N1", 0),
        ("R", 2), ("S5", 2), ("N2", 0), ("R", 3), ("S5", 3), ("N3", 0), ("R", 2), ("og", 0),
        ("R", 1), ("kvs", 0), ("S5", 4), ("N4", 0), ("R", 3), ("kvf", 0), ("as", 0), ("T0", 0),
        ("S5", 5), ("N5", 0), ("R", 3), ("as", 1), ("T0", 1), ("S5", 6), ("T1", 0), ("S5", 7),
        ("R", 3), ("kvs", 1), ("T2", 0), ("S5", 8), ("T1", 1), ("R", 1), ("kvf", 1), ("R", 1),
        ("S5", 9), ("T2", 1), ("T3", 0), ("R", 2), ("as", 2), ("T0", 2), ("S5", 10), ("R", 1),
        ("S5", 11), ("T1", 2), ("T3", 1), ("T4", 0), ("R", 2), ("kvs", 2), ("R", 1), ("kvf", 2),
        ("T2", 2), ("T5", 0), ("T4", 1), ("I", 0), ("I", 1), ("I", 2), ("R", 1), ("as", 3),
        ("T0", 3), ("I", 3), ("R", 2), ("T3", 2), ("F", 0), ("T5", 1), ("R", 1), ("T1", 3),
        ("T4", 2), ("R", 3), ("F", 1), ("F", 2), ("T5", 2), ("T2", 3), ("R", 2), ("T3", 3),
        ("R", 1), ("F", 3), ("T4", 3), ("R", 4), ("T5", 3), ("R", 1),
    ]
    return plan + [("N%d" % n, 0) for n in range(6, doublings + 1)]


def results_kernel(y, dx, mlp, out, qkv, ga, gm, y2, dx2, gate2, up2, down2, out2, qkv2, ga2, gm2,
                   low, wide, held, in_sem, out_sem, row_sem):
    width, qw = mlp.shape[1], out.shape[0]
    half = width // 2
    pairs = []
    for n, dst in enumerate((gate2, up2, down2)):
        for p in range(2):
            rows = pl.ds(p * half, half)
            pairs.append((mlp.at[n, rows], dst.at[rows], half))
    for n in range(3):
        pairs.append((qkv.at[n], qkv2.at[n], qw))
    pairs.append((out, out2, qw))
    moves = []
    at = 0
    for k, (src, dst, size) in enumerate(pairs):
        part = pl.ds(at, size)
        moves.append((
            pltpu.make_async_copy(src, low.at[part], in_sem.at[k]),
            pltpu.make_async_copy(wide.at[part], dst, out_sem.at[k]),
            slice(at, at + size),
        ))
        at += size
    rows = [
        (
            pltpu.make_async_copy(src, held.at[n], row_sem.at[n]),
            pltpu.make_async_copy(held.at[n], dst, row_sem.at[2 + n]),
        )
        for n, (src, dst) in enumerate(((y, y2), (dx, dx2)))
    ]
    for load, _, _ in moves:
        load.start()
    for load, _ in rows:
        load.start()
    ga2[...] = ga[0]
    gm2[...] = gm[0]
    for load, store, part in moves:
        load.wait()
        wide[part, :] = low[part, :].astype(f32)
        store.start()
    for load, store in rows:
        load.wait()
        store.start()
    for _, store, _ in moves:
        store.wait()
    for _, store in rows:
        store.wait()


def results(y, dx, g_mlp, g_out, g_qkv, g_ga, g_gm):
    _, width, fq = g_mlp.shape
    qw = g_out.shape[0]
    total = 3 * width + 4 * qw
    vmem = pl.BlockSpec(memory_space=pltpu.VMEM)
    hbm = pl.BlockSpec(memory_space=pl.ANY)
    S = jax.ShapeDtypeStruct
    dma = pltpu.SemaphoreType.DMA
    return pl.pallas_call(
        results_kernel,
        out_shape=[
            S(y.shape, bf16), S(dx.shape, bf16), S((width, fq), f32), S((width, fq), f32),
            S((fq, width), f32), S((qw, width), f32), S((3, qw, width), f32),
            S((width,), f32), S((width,), f32),
        ],
        in_specs=[hbm] * 5 + [vmem] * 2,
        out_specs=[hbm] * 7 + [vmem] * 2,
        scratch_shapes=[
            pltpu.VMEM((total, width), bf16), pltpu.VMEM((total, width), f32),
            pltpu.VMEM((2, *y.shape), bf16), dma((10,)), dma((10,)), dma((4,)),
        ],
        compiler_params=pltpu.CompilerParams(vmem_limit_bytes=VLIM),
    )(y, dx, g_mlp, g_out, g_qkv, g_ga, g_gm)


def on_device(
    nrows, tokens, lengths, w_qkv, w_out, w_gate, w_up, w_down, gain_attn, gain_mlp, cotangent
):
    _, length, width = tokens.shape
    qw = w_qkv.shape[2]
    fq = w_gate.shape[1]
    hc = qw // HEAD
    nh = 2 * hc
    cl = length // NCH
    tq = 2 * cl
    ntok = 2 * length
    nkey = 2 * ntok
    cores, chunk, xs, place = np.meshgrid(
        np.arange(2), np.arange(NCH), np.arange(2), np.arange(cl), indexing="ij"
    )
    position = ((2 * xs + cores) * length + chunk * cl + place).reshape(2, ntok)
    half = HEAD // 2
    freqs = rope_base ** (-np.arange(half) / half)
    angles = freqs[None, :, None] * position[:, None, :]
    turns = np.stack([np.cos(angles), np.sin(angles)], axis=1).astype(np.float32)
    places = position.reshape(1, nkey).astype(np.int32)

    hbm = pl.BlockSpec(memory_space=pl.ANY)
    vmem = pl.BlockSpec(memory_space=pltpu.VMEM)
    S = jax.ShapeDtypeStruct
    V = pltpu.VMEM
    dma = pltpu.SemaphoreType.DMA
    doublings = 2 + (nrows - 1).bit_length()
    scratch = [
        V((NCH, 2, cl, width), bf16),
        V((length, width), bf16),
        V((2, hc, 3, HEAD, width), bf16),
        V((2, hc, 2, HEAD, width), bf16),
        V((9, width, fq), bf16),
        V((hc, 2, 2 * HEAD, nkey), bf16),
        V((hc, 2, 2 * HEAD, nkey), bf16),
        V((2, hc, ntok, 2 * HEAD), bf16),
        V((2, hc, HEAD, ntok), bf16),
        V((2, ntok, 2 * qw), bf16),
        V((ntok, width), bf16),
        V((length, width), f32),
        V((length, width), f32),
        V((length, 128), f32),
        V((2 * ntok, fq), bf16),
        V((2 * ntok, fq), bf16),
        V((2 * ntok, fq), bf16),
        V((NCH, 2, cl, width), bf16),
        V((NCH, 2, cl, width), bf16),
        V((NCH, cl, width), bf16),
        V((NCH, cl, width), bf16),
        V((NCH, cl, width), bf16),
        V((NCH, cl, width), bf16),
        V((2, cl, width), f32),
        V((2, cl, 128), f32),
        V((2, 2, 2 * HEAD, nkey), f32),
        V((hc, 2, 2 * HEAD, ntok), bf16),
        V((2, 3 * qw, ntok), bf16),
        V((NCH, cl, width), bf16),
        V(((1 + hc) * 3 * HEAD, width), bf16),
        V((8, width), f32),
        V((doublings, 8, width), f32),
        V((2, HEAD // 2, ntok), f32),
        dma((NCH + 9,)),
        dma((3,)), dma((3,)),
        dma((7,)), dma((7,)),
        dma((NCH,)), dma((NCH,)),
        dma((NCH, 4)), dma((NCH, 4)),
        dma((NCH,)), dma((NCH,)),
        dma((NCH,)), dma((NCH,)),
        dma((NCH,)), dma((NCH,)),
        dma((NCH,)), dma((NCH,)),
        dma((NCH,)), dma((NCH,)),
        dma((hc,)), dma((hc,)),
        dma((NCH,)), dma((NCH,)),
        dma((4 + hc,)), dma((4 + hc,)), dma((3 + 3 * hc,)),
        dma((3, 2, 14)), dma((3, 2, 14)),
        dma((1 + hc, 5)), dma((1 + hc, 5)),
        dma((doublings,)), dma((doublings,)),
        dma((NCH,)),
        pltpu.SemaphoreType.REGULAR((4,)),
    ]
    outs = pl.pallas_call(
        functools.partial(layer_kernel, nrows),
        out_shape=[
            S((length, width), bf16), S((length, width), bf16),
            S((3, width, fq), bf16), S((qw, width), bf16), S((3, hc, HEAD, width), bf16),
            S((1, width), f32), S((1, width), f32),
        ],
        in_specs=[hbm] * 8 + [pl.BlockSpec(memory_space=pltpu.SMEM)] + [vmem] * 3,
        out_specs=[hbm] * 5 + [vmem] * 2,
        scratch_shapes=scratch,
        compiler_params=pltpu.CompilerParams(
            collective_id=0, has_side_effects=True, vmem_limit_bytes=VLIM
        ),
    )(
        tokens[0], cotangent[0],
        w_qkv.transpose(0, 2, 1).reshape(3, hc, HEAD, width), w_out.reshape(hc, HEAD, width), w_gate, w_up, w_down,
        jnp.asarray(turns), lengths, gain_attn, gain_mlp, jnp.asarray(places),
    )
    y, dx, g_mlp, g_out, g_qkv, g_ga, g_gm = outs
    if nrows != 8:
        g_mlp, g_out, g_qkv = lax.psum((g_mlp, g_out, g_qkv), "rows")
    y, dx, gate2, up2, down2, out2, qkv2, g_ga, g_gm = results(
        y, dx, g_mlp, g_out, g_qkv.reshape(3, qw, width), g_ga, g_gm
    )
    return (
        y[None], dx[None], qkv2.transpose(0, 2, 1), out2, gate2, up2, down2, g_ga, g_gm,
    )


VLIM = 64 * 2**20


def solution(mesh):
    in_specs = (
        P("rows", "heads", None),
        P("rows"),
        P(None, None, "heads"),
        P("heads", None),
        P(None, "heads"),
        P(None, "heads"),
        P("heads", None),
        P(),
        P(),
        P("rows", "heads", None),
    )
    out_specs = (
        P("rows", "heads", None),
        P("rows", "heads", None),
        P(None, None, "heads"),
        P("heads", None),
        P(None, "heads"),
        P(None, "heads"),
        P("heads", None),
        P(),
        P(),
    )
    return jax.shard_map(
        functools.partial(on_device, mesh.shape["rows"]), mesh=mesh, in_specs=in_specs, out_specs=out_specs, check_vma=False
    )
```
